256 devices in a mesh: dom: 8 (over x_hi, y), slab: 32 (over z, x_lo, core).
Axes of the slice: x: 4 (x_hi: 2, x_lo: 2; x = x_hi * 2 + x_lo), y: 4, z: 8, core: 2. Of those that a mesh axis runs over, the one named last changes fastest.
Arguments:
- images: bfloat16 [2048, 256, 512], P(('dom', 'slab')), may hold values from -6 to 6
- orient_ids: int32 [2048], P(('dom', 'slab')), may hold values from 0 to 5
- shift_ids: int32 [2048], P(('dom', 'slab')), may hold values from 0 to 15
- group_ids: int32 [2048], P(('dom', 'slab')), may hold values from 0 to 7
- translations: float32 [16, 2], replicated, may hold values from -6 to 6
- defocus: float32 [8], replicated, may hold values from 2 to 24
- in_plane: bfloat16 [6, 256, 256], replicated, may hold values from -0.375 to 0.375
- slab_rows: bfloat16 [6, 256, 256, 256], P(None, 'slab'), may hold values from -0.15625 to 0.15625
Outputs:
- density: float32 [256, 256, 256], P('slab', 'dom')
The draws below stay inside these ranges and needn't reach their ends.
All inputs are finite; a program needn't handle non-finite values.
Results may differ from the reference program's by a relative error of at most 0.007.
Values may be sent and summed in bfloat16 or wider, within the bound.
No kernel may reach another device: no remote copies, remote signals or barrier semaphores. Data moves between devices by JAX's collectives and lax.ppermute only.
A program may use at most 64 MiB of HBM per device.

```python
import math
import jax
import jax.numpy as jnp
from jax import lax

N = 256
ORIENT = 6
NTRANS = 16
NGROUP = 8
IMG_DEV = 8
PARTS_SIZE = 2048
N_DOM = 8
N_SLAB = 32


def place_ends(values, key, smallest, high):
    dims = values.shape
    index_at = [jax.random.randint(jax.random.fold_in(key, axis), (), 0, dims[axis]) for axis in range(len(dims))]
    values = values.at[tuple(index_at)].set(smallest)
    longest = dims.index(max(dims))
    index_at[longest] = (index_at[longest] + 1) % dims[longest]
    return values.at[tuple(index_at)].set(high)


def block_levels(stream_key, dims, split, smallest, top_value):
    factor_of, own = 1.0, jax.random.fold_in(stream_key, 6)
    for dim, blocks in split:
        steps = jnp.exp(jax.random.uniform(jax.random.fold_in(own, dim), (blocks,), jnp.float32, smallest / len(split), top_value / len(split)))
        factor_of = factor_of * jnp.repeat(steps, dims[dim] // blocks).reshape([-1 if axis == dim else 1 for axis in range(len(dims))])
    return factor_of


def normal_values(key, shape, deviation, bound, pieces=(), held_as=jnp.bfloat16):
    gain = block_levels(key, shape, pieces, -0.22, 0.18) if pieces else 1.0
    values = jax.random.normal(key, shape, jnp.float32) * deviation * gain
    return jnp.minimum(jnp.maximum(values, -bound), bound).astype(held_as)


def setup_inputs(seed: int = 0) -> dict:
    seeds = jax.random.split(jax.random.key(seed), 9)
    return {
        "images": normal_values(seeds[0], (PARTS_SIZE, N, 2 * N), 1.0, 6.0, ((0, 256),)),
        "orient_ids": place_ends(jax.random.randint(seeds[1], (PARTS_SIZE,), 0, ORIENT), jax.random.fold_in(seeds[1], 1), 0, ORIENT - 1).astype(jnp.int32),
        "shift_ids": place_ends(jax.random.randint(seeds[2], (PARTS_SIZE,), 0, NTRANS), jax.random.fold_in(seeds[2], 1), 0, NTRANS - 1).astype(jnp.int32),
        "group_ids": place_ends(jax.random.randint(seeds[3], (PARTS_SIZE,), 0, NGROUP), jax.random.fold_in(seeds[3], 1), 0, NGROUP - 1).astype(jnp.int32),
        "translations": jnp.clip(jax.random.uniform(seeds[4], (NTRANS, 2), jnp.float32, -6.0, 6.0), -6.0, 6.0),
        "defocus": jnp.clip(jnp.exp(jax.random.uniform(seeds[5], (NGROUP,), jnp.float32, math.log(2.0), math.log(24.0))), 2.0, 24.0),
        "in_plane": normal_values(seeds[6], (ORIENT, N, N), N ** -0.5, 0.375),
        "slab_rows": normal_values(seeds[7], (ORIENT, N, N, N), (ORIENT * N) ** -0.5, 0.15625, ((1, 32),)),
    }


def frequencies(length):
    position = jnp.arange(length, dtype=jnp.int32)
    return jnp.where(position < length // 2, position, position - length).astype(jnp.float32)

def weight_images(images, shifts, focus_values):
    length = images.shape[1]
    frequency = frequencies(length)
    radius = (frequency[:, None] ** 2 + frequency[None, :] ** 2) / float((length // 2) ** 2)
    phase_angle = 2.0 * math.pi / length * (shifts[:, 0, None, None] * frequency[None, :, None] + shifts[:, 1, None, None] * frequency[None, None, :])
    contrast = -jnp.sin(focus_values[:, None, None] * radius[None] + 0.1)
    real_part = images[:, :, :length].astype(jnp.float32)
    imag_part = images[:, :, length:].astype(jnp.float32)
    cosine = jnp.cos(phase_angle)
    sine_table = jnp.sin(phase_angle)
    return jnp.concatenate([contrast * (real_part * cosine + imag_part * sine_table), contrast * (imag_part * cosine - real_part * sine_table)], axis=2)

def mix_columns(class_total, in_plane):
    classes, row_count, columns = class_total.shape
    halves = class_total.astype(jnp.float32).reshape(classes, row_count, 2, columns // 2)
    product = jnp.einsum('okrx,oxw->okrw', halves, in_plane.astype(jnp.float32), precision=lax.Precision.HIGHEST)
    return product.astype(jnp.bfloat16).reshape(classes, row_count, columns)

def reference(images, orient_ids, shift_ids, group_ids, translations, defocus, in_plane, slab_rows):
    group_size = IMG_DEV * N_SLAB

    def one_group(group_index):
        first_row = group_index * group_size
        block_images = lax.dynamic_slice_in_dim(images, first_row, group_size, 0)
        orients = lax.dynamic_slice_in_dim(orient_ids, first_row, group_size, 0)
        shifts = translations[lax.dynamic_slice_in_dim(shift_ids, first_row, group_size, 0)]
        focus_values = defocus[lax.dynamic_slice_in_dim(group_ids, first_row, group_size, 0)]
        weighted = weight_images(block_images, shifts, focus_values)
        class_total = jax.ops.segment_sum(weighted, orients, num_segments=ORIENT)
        return mix_columns(class_total.astype(jnp.bfloat16), in_plane).astype(jnp.float32)
    mixed_rows = lax.optimization_barrier(jnp.sum(lax.map(one_group, jnp.arange(N_DOM, dtype=jnp.int32)), axis=0))
    plane_block = min(16, N)

    def insert_block(block_index):
        planes = lax.dynamic_slice_in_dim(slab_rows, block_index * plane_block, plane_block, 1).astype(jnp.float32)
        return jnp.einsum('ozyk,okc->zyc', planes, mixed_rows, precision=lax.Precision.HIGHEST)
    spectrum = lax.map(insert_block, jnp.arange(N // plane_block, dtype=jnp.int32)).reshape(N, N, 2 * N)
    complex_spectrum = spectrum[:, :, :N] + 1j * spectrum[:, :, N:]
    real_space = jnp.real(jnp.fft.ifftn(complex_spectrum)) * (N ** 1.5 / math.sqrt(PARTS_SIZE))
    return jnp.transpose(real_space, (2, 1, 0)).astype(jnp.float32)
```

```python
import math

import jax
import jax.numpy as jnp
import numpy as np
from jax import lax
from jax.experimental import pallas as pl
from jax.experimental.pallas import tpu as pltpu
from jax.sharding import Mesh
from jax.sharding import PartitionSpec as P

N = 256
ORIENT = 6
IMG = 8
BF16 = jnp.bfloat16
F32 = jnp.float32

DOM = ("xh", "yy")
SLAB = ("zz", "xl", "co")
ALL = DOM + SLAB


def split_table(table):
    high = table.astype(jnp.bfloat16)
    low = (table - high.astype(np.float64)).astype(jnp.bfloat16)
    return high, low


def phases(left, right):
    angles = (np.outer(left, right) % N) * (2.0 * math.pi / N)
    return np.cos(angles), np.sin(angles)


def x_table():
    x_of = (8 * np.arange(32)[None, :] + np.arange(8)[:, None]).reshape(-1)
    cosine, sine = (t.reshape(8, 32, N) for t in phases(x_of, np.arange(N)))
    real_rows = np.concatenate([cosine, -sine], axis=2)
    imag_rows = np.concatenate([sine, cosine], axis=2)
    return split_table(np.stack([real_rows, imag_rows], axis=1).reshape(512, 512))


def y_table():
    cosine, sine = (t.reshape(N, 8, 32) for t in phases(np.arange(N), np.arange(N)))
    from_real = np.stack([cosine, sine], axis=2).reshape(N, 512)
    from_imag = np.stack([-sine, cosine], axis=2).reshape(N, 512)
    return split_table(np.concatenate([from_real, from_imag], axis=0))


def z_table():
    half, slab, part = np.meshgrid(np.arange(2), np.arange(32), np.arange(4), indexing="ij")
    kz_of = (8 * slab + 4 * half + part).reshape(-1)
    cosine, sine = (t.reshape(2, 128, N) for t in phases(kz_of, np.arange(N)))
    return split_table(np.stack([cosine, -sine], axis=1).reshape(512, N))


def rows_dot(left, right):
    return lax.dot_general(left, right, (((1,), (1,)), ((), ())), preferred_element_type=F32)


def plain_dot(left, right):
    return jnp.dot(left, right, preferred_element_type=F32)


def front_kernel(
    orient, shift, group, trans, defocus, core, images, in_plane, x_high, x_low, keep, send, total
):
    position = lax.broadcasted_iota(jnp.int32, (IMG, N), 1)
    freq = jnp.where(position < N // 2, position, position - N).astype(F32)
    row = lax.broadcasted_iota(jnp.int32, (IMG, N), 0)
    shift_y = jnp.zeros((IMG, N), F32)
    shift_x = jnp.zeros((IMG, N), F32)
    focus = jnp.zeros((IMG, N), F32)
    for p in range(IMG):
        shift_y = jnp.where(row == p, trans[shift[p], 0], shift_y)
        shift_x = jnp.where(row == p, trans[shift[p], 1], shift_x)
        focus = jnp.where(row == p, defocus[group[p]], focus)
    squares = freq * freq * (1.0 / (N // 2) ** 2)
    step = 2.0 * math.pi / N
    angles = jnp.concatenate(
        [
            step * shift_y * freq,
            focus * squares + 0.1,
            step * shift_x * freq,
            focus * squares,
        ],
        axis=0,
    )
    sines = jnp.sin(angles)
    cosines = jnp.cos(angles)
    columns = jnp.concatenate([sines, cosines, jnp.zeros((64, N), F32)], axis=0).T
    total[...] = jnp.zeros_like(total)
    chunk = 32
    for p in range(IMG):
        sin_tx, sin_fx = sines[16 + p : 17 + p], sines[24 + p : 25 + p]
        cos_tx, cos_fx = cosines[16 + p : 17 + p], cosines[24 + p : 25 + p]
        which = orient[p]
        for r in range(0, N, chunk):
            rows = slice(r, r + chunk)
            sin_ty = columns[rows, p : p + 1]
            sin_fy = columns[rows, 8 + p : 9 + p]
            cos_ty = columns[rows, 32 + p : 33 + p]
            cos_fy = columns[rows, 40 + p : 41 + p]
            contrast = -(sin_fy * cos_fx + cos_fy * sin_fx)
            turn_re = contrast * (cos_ty * cos_tx - sin_ty * sin_tx)
            turn_im = contrast * (sin_ty * cos_tx + cos_ty * sin_tx)
            real_part = images[p, rows, :N].astype(F32)
            imag_part = images[p, rows, N:].astype(F32)
            total[which, rows, :N] += real_part * turn_re + imag_part * turn_im
            total[which, rows, N:] += imag_part * turn_re - real_part * turn_im
    first = core[0] == 0
    for o in range(ORIENT):
        sums = total[o].astype(BF16)
        matrix = in_plane[o]
        mixed = jnp.concatenate(
            [plain_dot(sums[:, :N], matrix), plain_dot(sums[:, N:], matrix)], axis=1
        ).astype(BF16)
        along = rows_dot(x_high[...], mixed) + rows_dot(x_low[...], mixed)
        along = along.astype(BF16)
        low_half, high_half = along[:, :128], along[:, 128:]
        own = jnp.where(first, low_half, high_half)
        other = jnp.where(first, high_half, low_half)
        for d in range(8):
            keep[d, 64 * o : 64 * o + 64, :] = own[64 * d : 64 * d + 64]
            send[d, 64 * o : 64 * o + 64, :] = other[64 * d : 64 * d + 64]


def insert_kernel(gathered, slab_rows, y_high, y_low, out, rows_all, spectrum):
    plane = pl.program_id(0)

    @pl.when(plane == 0)
    def _():
        for i in range(16):
            for c in range(2):
                rows_all[24 * i : 24 * i + 24, 128 * c : 128 * c + 128] = gathered[
                    2 * i + c
                ].astype(F32)

    found = jnp.zeros((64, N), F32)
    for o in range(ORIENT):
        found += rows_dot(rows_all[64 * o : 64 * o + 64, :].astype(BF16), slab_rows[o, 0])
    start = (plane // 4) * 128 + plane % 4
    for part in range(4):
        rows, lanes = 32 * (part // 2), 128 * (part % 2)
        spectrum[part, pl.ds(start, 32, stride=4), :] = found[rows : rows + 32, lanes : lanes + 128]

    @pl.when(plane == pl.num_programs(0) - 1)
    def _():
        lane = lax.broadcasted_iota(jnp.int32, (128, 128), 1)
        both = jnp.concatenate([spectrum[part] for part in range(4)], axis=1).astype(BF16)
        result = plain_dot(both, y_high[...]) + plain_dot(both, y_low[...])
        for e in range(4):
            early = result[:128, 128 * e : 128 * e + 128]
            late = result[128:, 128 * e : 128 * e + 128]
            even = jnp.where(lane < 64, early, pltpu.roll(late, 64, 1))
            odd = jnp.where(lane < 64, pltpu.roll(early, 64, 1), late)
            out[2 * e] = even.astype(BF16)
            out[2 * e + 1] = odd.astype(BF16)


def last_kernel(pencils, z_high, z_low, out):
    scaling = 1.0 / (N**1.5 * math.sqrt(2048))
    rows = []
    for d in range(8):
        turned = pencils[d].astype(F32).T.astype(BF16)
        rows.append(jnp.concatenate([turned[32 * q : 32 * q + 32] for q in range(4)], axis=1))
    stacked = jnp.concatenate(rows, axis=0)
    result = plain_dot(stacked, z_high[...]) + plain_dot(stacked, z_low[...])
    for d in range(8):
        out[d] = result[32 * d : 32 * d + 32] * scaling


VMEM_SPEC = pl.BlockSpec(memory_space=pltpu.VMEM)
SMEM_SPEC = pl.BlockSpec(memory_space=pltpu.SMEM)
LIMIT = 48 * 1024 * 1024


def on_device(images, orient_ids, shift_ids, group_ids, translations, defocus, in_plane, slab_rows):
    core = lax.axis_index("co").astype(jnp.int32).reshape(1)
    x_high, x_low = x_table()
    keep, send = pl.pallas_call(
        front_kernel,
        out_shape=[jax.ShapeDtypeStruct((8, 384, 128), BF16)] * 2,
        in_specs=[SMEM_SPEC] * 6 + [VMEM_SPEC] * 4,
        out_specs=[VMEM_SPEC] * 2,
        scratch_shapes=[pltpu.VMEM((ORIENT, N, 2 * N), F32)],
        compiler_params=pltpu.CompilerParams(vmem_limit_bytes=LIMIT),
        name="front",
    )(
        orient_ids, shift_ids, group_ids, translations, defocus, core,
        images, in_plane, jnp.asarray(x_high), jnp.asarray(x_low),
    )
    other = lax.ppermute(send, "co", [(0, 1), (1, 0)])
    pair = (keep.astype(F32) + other.astype(F32)).astype(BF16)
    pieces = lax.all_to_all(pair, DOM, split_axis=0, concat_axis=0, tiled=True)
    part = jnp.sum(pieces.astype(F32), axis=0).astype(BF16)
    pieces = lax.all_to_all(
        part.reshape(16, 24, 128), ("zz", "xl"), split_axis=0, concat_axis=0, tiled=True
    )
    part = jnp.sum(pieces.astype(F32), axis=0).astype(BF16)
    gathered = lax.all_to_all(
        jnp.broadcast_to(part[None], (32, 24, 128)), SLAB, split_axis=0, concat_axis=0, tiled=True
    )
    y_high, y_low = y_table()
    planes = slab_rows.shape[1]
    sent = pl.pallas_call(
        insert_kernel,
        out_shape=jax.ShapeDtypeStruct((8, 128, 128), BF16),
        grid=(planes,),
        in_specs=[
            pl.BlockSpec((32, 24, 128), lambda i: (0, 0, 0)),
            pl.BlockSpec((ORIENT, 1, N, N), lambda i: (0, i, 0, 0)),
            pl.BlockSpec((512, 512), lambda i: (0, 0)),
            pl.BlockSpec((512, 512), lambda i: (0, 0)),
        ],
        out_specs=pl.BlockSpec((8, 128, 128), lambda i: (0, 0, 0)),
        scratch_shapes=[pltpu.VMEM((384, N), F32), pltpu.VMEM((4, N, 128), F32)],
        compiler_params=pltpu.CompilerParams(vmem_limit_bytes=LIMIT),
        name="insert",
    )(gathered, slab_rows, jnp.asarray(y_high), jnp.asarray(y_low))
    pencils = lax.all_to_all(
        sent.reshape(256, 4, 128), ALL, split_axis=0, concat_axis=0, tiled=True
    )
    z_high, z_low = z_table()
    return pl.pallas_call(
        last_kernel,
        out_shape=jax.ShapeDtypeStruct((8, 32, N), F32),
        in_specs=[VMEM_SPEC] * 3,
        out_specs=VMEM_SPEC,
        compiler_params=pltpu.CompilerParams(vmem_limit_bytes=LIMIT),
        name="last",
    )(pencils.reshape(8, 128, 128), jnp.asarray(z_high), jnp.asarray(z_low))


def solution(mesh):
    fine = Mesh(mesh.devices.reshape(2, 4, 8, 2, 2), ALL)
    return jax.shard_map(
        on_device,
        mesh=fine,
        in_specs=(
            P(ALL, None, None),
            P(ALL),
            P(ALL),
            P(ALL),
            P(),
            P(),
            P(),
            P(None, SLAB, None, None),
        ),
        out_specs=P(SLAB, DOM, None),
        check_vma=False,
    )
```

```python
import math

import jax
import jax.numpy as jnp
import numpy as np
from jax import lax
from jax.experimental import pallas as pl
from jax.experimental.pallas import tpu as pltpu
from jax.sharding import Mesh
from jax.sharding import PartitionSpec as P

N = 256
ORIENT = 6
IMG = 8
BF16 = jnp.bfloat16
F32 = jnp.float32

DOM = ("xh", "yy")
SLAB = ("zz", "xl", "co")
ALL = DOM + SLAB


def split_table(table):
    high = table.astype(jnp.bfloat16)
    low = (table - high.astype(np.float64)).astype(jnp.bfloat16)
    return high, low


def phases(left, right):
    angles = (np.outer(left, right) % N) * (2.0 * math.pi / N)
    return np.cos(angles), np.sin(angles)


def x_table():
    x_of = (8 * np.arange(32)[None, :] + np.arange(8)[:, None]).reshape(-1)
    cosine, sine = (t.reshape(8, 32, N) for t in phases(x_of, np.arange(N)))
    real_rows = np.concatenate([cosine, -sine], axis=2)
    imag_rows = np.concatenate([sine, cosine], axis=2)
    return split_table(np.stack([real_rows, imag_rows], axis=1).reshape(512, 512))


def y_table():
    cosine, sine = (t.reshape(N, 8, 32) for t in phases(np.arange(N), np.arange(N)))
    from_real = np.stack([cosine, sine], axis=2).reshape(N, 512)
    from_imag = np.stack([-sine, cosine], axis=2).reshape(N, 512)
    return split_table(np.concatenate([from_real, from_imag], axis=0))


def z_table():
    half, slab, part = np.meshgrid(np.arange(2), np.arange(32), np.arange(4), indexing="ij")
    kz_of = (8 * slab + 4 * half + part).reshape(-1)
    cosine, sine = (t.reshape(2, 128, N) for t in phases(kz_of, np.arange(N)))
    return split_table(np.stack([cosine, -sine], axis=1).reshape(512, N))


def rows_dot(left, right):
    return lax.dot_general(left, right, (((1,), (1,)), ((), ())), preferred_element_type=F32)


def plain_dot(left, right):
    return jnp.dot(left, right, preferred_element_type=F32)


def front_kernel(
    scalars, images_hbm, in_plane_hbm, x_hbm,
    keep, send,
    total, images, in_plane, x_both, big_sems, image_sems,
):
    image_copies = [
        pltpu.make_async_copy(images_hbm.at[p], images.at[p], image_sems.at[p]) for p in range(IMG)
    ]
    for copy in image_copies:
        copy.start()
    plane_copy = pltpu.make_async_copy(in_plane_hbm, in_plane, big_sems.at[0])
    table_copy = pltpu.make_async_copy(x_hbm, x_both, big_sems.at[1])
    plane_copy.start()
    table_copy.start()
    total[...] = jnp.zeros_like(total)
    position = lax.broadcasted_iota(jnp.int32, (IMG, N), 1)
    freq = jnp.where(position < N // 2, position, position - N).astype(F32)
    row = lax.broadcasted_iota(jnp.int32, (IMG, N), 0)
    shift_y = jnp.zeros((IMG, N), F32)
    shift_x = jnp.zeros((IMG, N), F32)
    focus = jnp.zeros((IMG, N), F32)
    classes = []
    for p in range(IMG):
        code = scalars[p].astype(jnp.int32)
        shift, group = (code // 8) % 16, code // 128
        classes.append(code % 8)
        shift_y = jnp.where(row == p, scalars[8 + shift], shift_y)
        shift_x = jnp.where(row == p, scalars[24 + shift], shift_x)
        focus = jnp.where(row == p, scalars[40 + group], focus)
    squares = freq * freq * (1.0 / (N // 2) ** 2)
    step = 2.0 * math.pi / N
    angles = jnp.concatenate(
        [
            step * shift_y * freq,
            focus * squares + 0.1,
            step * shift_x * freq,
            focus * squares,
        ],
        axis=0,
    )
    sines = jnp.sin(angles)
    cosines = jnp.cos(angles)
    columns = jnp.concatenate([sines, cosines, jnp.zeros((64, N), F32)], axis=0).T
    chunk = 32
    for p in range(IMG):
        sin_tx, sin_fx = sines[16 + p : 17 + p], sines[24 + p : 25 + p]
        cos_tx, cos_fx = cosines[16 + p : 17 + p], cosines[24 + p : 25 + p]
        which = classes[p]
        image_copies[p].wait()
        for r in range(0, N, chunk):
            rows = slice(r, r + chunk)
            sin_ty = columns[rows, p : p + 1]
            sin_fy = columns[rows, 8 + p : 9 + p]
            cos_ty = columns[rows, 32 + p : 33 + p]
            cos_fy = columns[rows, 40 + p : 41 + p]
            contrast = -(sin_fy * cos_fx + cos_fy * sin_fx)
            turn_re = contrast * (cos_ty * cos_tx - sin_ty * sin_tx)
            turn_im = contrast * (sin_ty * cos_tx + cos_ty * sin_tx)
            real_part = images[p, rows, :N].astype(F32)
            imag_part = images[p, rows, N:].astype(F32)
            total[which, rows, :N] += real_part * turn_re + imag_part * turn_im
            total[which, rows, N:] += imag_part * turn_re - real_part * turn_im
    first = lax.axis_index("co") == 0
    plane_copy.wait()
    table_copy.wait()
    for o in range(ORIENT):
        sums = total[o].astype(BF16)
        matrix = in_plane[o]
        mixed = jnp.concatenate(
            [plain_dot(sums[:, :N], matrix), plain_dot(sums[:, N:], matrix)], axis=1
        ).astype(BF16)
        along = (rows_dot(x_both[0], mixed) + rows_dot(x_both[1], mixed)).astype(BF16)
        low_half, high_half = along[:, :128], along[:, 128:]
        own = jnp.where(first, low_half, high_half)
        other = jnp.where(first, high_half, low_half)
        for d in range(8):
            keep[d, 64 * o : 64 * o + 64, :] = own[64 * d : 64 * d + 64]
            send[d, 64 * o : 64 * o + 64, :] = other[64 * d : 64 * d + 64]


def insert_kernel(own, across, beside, corner, slab_hbm, y_both, out, rows_all, spectrum, slab_rows, sems):
    copies = [
        pltpu.make_async_copy(slab_hbm.at[:, plane], slab_rows.at[:, plane], sems.at[plane])
        for plane in range(8)
    ]
    for copy in copies:
        copy.start()
    side, core = lax.axis_index("xl"), lax.axis_index("co")
    rows_all[side, core] = own[...]
    rows_all[side, 1 - core] = across[...]
    rows_all[1 - side, core] = beside[...]
    rows_all[1 - side, 1 - core] = corner[...]
    for plane in range(8):
        copies[plane].wait()
        found = jnp.zeros((64, N), F32)
        for o in range(ORIENT):
            rows = slice(64 * (o % 3), 64 * (o % 3) + 64)
            factor = jnp.concatenate([rows_all[o // 3, c, rows, :] for c in range(2)], axis=1)
            found += rows_dot(factor, slab_rows[o, plane])
        start = (plane // 4) * 128 + plane % 4
        for part in range(4):
            rows, lanes = 32 * (part // 2), 128 * (part % 2)
            spectrum[part, pl.ds(start, 32, stride=4), :] = found[
                rows : rows + 32, lanes : lanes + 128
            ]
    lane = lax.broadcasted_iota(jnp.int32, (128, 128), 1)
    both = jnp.concatenate([spectrum[part] for part in range(4)], axis=1).astype(BF16)
    result = plain_dot(both, y_both[0]) + plain_dot(both, y_both[1])
    for e in range(4):
        early = result[:128, 128 * e : 128 * e + 128]
        late = result[128:, 128 * e : 128 * e + 128]
        even = jnp.where(lane < 64, early, pltpu.roll(late, 64, 1))
        odd = jnp.where(lane < 64, pltpu.roll(early, 64, 1), late)
        out[2 * e] = even.astype(BF16)
        out[2 * e + 1] = odd.astype(BF16)


def last_kernel(pencils, z_high, z_low, out):
    scaling = 1.0 / (N**1.5 * math.sqrt(2048))
    rows = []
    for d in range(8):
        turned = pencils[d].astype(F32).T.astype(BF16)
        rows.append(jnp.concatenate([turned[32 * q : 32 * q + 32] for q in range(4)], axis=1))
    stacked = jnp.concatenate(rows, axis=0)
    result = plain_dot(stacked, z_high[...]) + plain_dot(stacked, z_low[...])
    for d in range(8):
        out[d] = result[32 * d : 32 * d + 32] * scaling


VMEM_SPEC = pl.BlockSpec(memory_space=pltpu.VMEM)
SMEM_SPEC = pl.BlockSpec(memory_space=pltpu.SMEM)
HBM_SPEC = pl.BlockSpec(memory_space=pltpu.HBM)
FRONT_LIMIT = 53500 * 1024
INSERT_LIMIT = 53000 * 1024
LAST_LIMIT = 32768 * 1024


def swap(array, bits):
    return lax.ppermute(array, ("xl", "co"), [(i, i ^ bits) for i in range(4)])


def total_of(pieces):
    return jnp.sum(pieces.astype(F32), axis=0).astype(BF16)


def on_device(images, orient_ids, shift_ids, group_ids, translations, defocus, in_plane, slab_rows):
    codes = orient_ids + 8 * shift_ids + 128 * group_ids
    scalars = jnp.concatenate([codes.astype(F32), translations[:, 0], translations[:, 1], defocus])
    keep, send = pl.pallas_call(
        front_kernel,
        out_shape=[
            jax.ShapeDtypeStruct((8, 384, 128), BF16),
            jax.ShapeDtypeStruct((8, 384, 128), BF16),
        ],
        in_specs=[SMEM_SPEC] + [HBM_SPEC] * 3,
        out_specs=[VMEM_SPEC] * 2,
        scratch_shapes=[
            pltpu.VMEM((ORIENT, N, 2 * N), F32),
            pltpu.VMEM((IMG, N, 2 * N), BF16),
            pltpu.VMEM((ORIENT, N, N), BF16),
            pltpu.VMEM((2, 512, 512), BF16),
            pltpu.SemaphoreType.DMA((2,)),
            pltpu.SemaphoreType.DMA((IMG,)),
        ],
        compiler_params=pltpu.CompilerParams(vmem_limit_bytes=FRONT_LIMIT),
        name="front",
    )(
        scalars, images, in_plane, jnp.asarray(np.stack(x_table())),
    )
    other = lax.ppermute(send, "co", [(0, 1), (1, 0)])
    pair = (keep.astype(F32) + other.astype(F32)).astype(BF16)
    pieces = lax.all_to_all(
        pair.reshape(16, 192, 128), DOM + ("xl",), split_axis=0, concat_axis=0, tiled=True
    )
    part = total_of(pieces)
    pieces = lax.all_to_all(
        jnp.broadcast_to(part[None], (8, 192, 128)), "zz", split_axis=0, concat_axis=0, tiled=True
    )
    own = total_of(pieces)
    sent = pl.pallas_call(
        insert_kernel,
        out_shape=jax.ShapeDtypeStruct((8, 128, 128), BF16),
        in_specs=[VMEM_SPEC] * 4 + [HBM_SPEC, VMEM_SPEC],
        out_specs=VMEM_SPEC,
        scratch_shapes=[
            pltpu.VMEM((2, 2, 192, 128), BF16),
            pltpu.VMEM((4, N, 128), F32),
            pltpu.VMEM((ORIENT, 8, N, N), BF16),
            pltpu.SemaphoreType.DMA((8,)),
        ],
        compiler_params=pltpu.CompilerParams(vmem_limit_bytes=INSERT_LIMIT),
        name="insert",
    )(own, swap(own, 1), swap(own, 2), swap(own, 3), slab_rows, jnp.asarray(np.stack(y_table())))
    pencils = lax.all_to_all(
        sent.reshape(256, 4, 128), ALL, split_axis=0, concat_axis=0, tiled=True
    )
    z_high, z_low = z_table()
    return pl.pallas_call(
        last_kernel,
        out_shape=jax.ShapeDtypeStruct((8, 32, N), F32),
        in_specs=[VMEM_SPEC] * 3,
        out_specs=VMEM_SPEC,
        compiler_params=pltpu.CompilerParams(vmem_limit_bytes=LAST_LIMIT),
        name="last",
    )(pencils.reshape(8, 128, 128), jnp.asarray(z_high), jnp.asarray(z_low))


def solution(mesh):
    fine = Mesh(mesh.devices.reshape(2, 4, 8, 2, 2), ALL)
    return jax.shard_map(
        on_device,
        mesh=fine,
        in_specs=(
            P(ALL, None, None),
            P(ALL),
            P(ALL),
            P(ALL),
            P(),
            P(),
            P(),
            P(None, SLAB, None, None),
        ),
        out_specs=P(SLAB, DOM, None),
        check_vma=False,
    )
```

```python
import math

import jax
import jax.numpy as jnp
import numpy as np
from jax import lax
from jax.experimental import pallas as pl
from jax.experimental.pallas import tpu as pltpu
from jax.sharding import Mesh
from jax.sharding import PartitionSpec as P

N = 256
ORIENT = 6
IMG = 8
BF16 = jnp.bfloat16
F32 = jnp.float32

DOM = ("xh", "yy")
SLAB = ("zz", "xl", "co")
ALL = DOM + SLAB


def split_table(table):
    high = table.astype(jnp.bfloat16)
    low = (table - high.astype(np.float64)).astype(jnp.bfloat16)
    return high, low


def phases(left, right):
    angles = (np.outer(left, right) % N) * (2.0 * math.pi / N)
    return np.cos(angles), np.sin(angles)


def x_table():
    x_of = (8 * np.arange(32)[None, :] + np.arange(8)[:, None]).reshape(-1)
    cosine, sine = (t.reshape(8, 32, N) for t in phases(x_of, np.arange(N)))
    real_rows = np.concatenate([cosine, -sine], axis=2)
    imag_rows = np.concatenate([sine, cosine], axis=2)
    return split_table(np.stack([real_rows, imag_rows], axis=1).reshape(512, 512))


def y_table():
    cosine, sine = (t.reshape(N, 8, 32) for t in phases(np.arange(N), np.arange(N)))
    from_real = np.stack([cosine, sine], axis=2).reshape(N, 512)
    from_imag = np.stack([-sine, cosine], axis=2).reshape(N, 512)
    return split_table(np.concatenate([from_real, from_imag], axis=0))


def z_table():
    half, slab, part = np.meshgrid(np.arange(2), np.arange(32), np.arange(4), indexing="ij")
    kz_of = (8 * slab + 4 * half + part).reshape(-1)
    cosine, sine = (t.reshape(2, 128, N) for t in phases(kz_of, np.arange(N)))
    return split_table(np.stack([cosine, -sine], axis=1).reshape(512, N))


def rows_dot(left, right):
    return lax.dot_general(left, right, (((1,), (1,)), ((), ())), preferred_element_type=F32)


def plain_dot(left, right):
    return jnp.dot(left, right, preferred_element_type=F32)


def front_kernel(
    scalars, images_hbm, in_plane_hbm, tables,
    keep, send,
    total, images, in_plane, x_rows, big_sems, image_sems,
):
    image_copies = [
        pltpu.make_async_copy(images_hbm.at[p], images.at[p], image_sems.at[p]) for p in range(IMG)
    ]
    for copy in image_copies:
        copy.start()
    plane_copy = pltpu.make_async_copy(in_plane_hbm, in_plane, big_sems.at[0])
    table_copy = pltpu.make_async_copy(tables.at[0], x_rows, big_sems.at[1])
    total[...] = jnp.zeros_like(total)
    position = lax.broadcasted_iota(jnp.int32, (IMG, N), 1)
    freq = jnp.where(position < N // 2, position, position - N).astype(F32)
    row = lax.broadcasted_iota(jnp.int32, (IMG, N), 0)
    shift_y = jnp.zeros((IMG, N), F32)
    shift_x = jnp.zeros((IMG, N), F32)
    focus = jnp.zeros((IMG, N), F32)
    classes = []
    for p in range(IMG):
        code = scalars[0, 16 + p].astype(jnp.int32)
        shift, group = (code // 8) % 16, code // 128
        classes.append(code % 8)
        shift_y = jnp.where(row == p, scalars[0, shift], shift_y)
        shift_x = jnp.where(row == p, scalars[1, shift], shift_x)
        focus = jnp.where(row == p, scalars[0, 24 + group], focus)
    squares = freq * freq * (1.0 / (N // 2) ** 2)
    step = 2.0 * math.pi / N
    angles = jnp.concatenate(
        [
            step * shift_y * freq,
            focus * squares + 0.1,
            step * shift_x * freq,
            focus * squares,
        ],
        axis=0,
    )
    sines = jnp.sin(angles)
    cosines = jnp.cos(angles)
    columns = jnp.concatenate([sines, cosines, jnp.zeros((64, N), F32)], axis=0).T
    for copy in image_copies:
        copy.wait()
    plane_copy.start()
    table_copy.start()
    chunk = 32
    for p in range(IMG):
        sin_tx, sin_fx = sines[16 + p : 17 + p], sines[24 + p : 25 + p]
        cos_tx, cos_fx = cosines[16 + p : 17 + p], cosines[24 + p : 25 + p]
        which = classes[p]
        for r in range(0, N, chunk):
            rows = slice(r, r + chunk)
            sin_ty = columns[rows, p : p + 1]
            sin_fy = columns[rows, 8 + p : 9 + p]
            cos_ty = columns[rows, 32 + p : 33 + p]
            cos_fy = columns[rows, 40 + p : 41 + p]
            contrast = -(sin_fy * cos_fx + cos_fy * sin_fx)
            turn_re = contrast * (cos_ty * cos_tx - sin_ty * sin_tx)
            turn_im = contrast * (sin_ty * cos_tx + cos_ty * sin_tx)
            real_part = images[p, rows, :N].astype(F32)
            imag_part = images[p, rows, N:].astype(F32)
            total[which, rows, :N] += real_part * turn_re + imag_part * turn_im
            total[which, rows, N:] += imag_part * turn_re - real_part * turn_im
    first = lax.axis_index("co") == 0
    plane_copy.wait()
    table_copy.wait()
    for o in range(ORIENT):
        sums = total[o].astype(BF16)
        matrix = in_plane[o]
        mixed = jnp.concatenate(
            [plain_dot(sums[:, :N], matrix), plain_dot(sums[:, N:], matrix)], axis=1
        ).astype(BF16)
        along = rows_dot(x_rows[...], mixed).astype(BF16)
        low_half, high_half = along[:, :128], along[:, 128:]
        own = jnp.where(first, low_half, high_half)
        other = jnp.where(first, high_half, low_half)
        for d in range(8):
            keep[d, 64 * o : 64 * o + 64, :] = own[64 * d : 64 * d + 64]
            send[d, 64 * o : 64 * o + 64, :] = other[64 * d : 64 * d + 64]


def fetch_kernel(after, slab_hbm, slab_rows, sems):
    del after
    copies = [
        pltpu.make_async_copy(slab_hbm.at[o], slab_rows.at[o], sems.at[o]) for o in range(ORIENT)
    ]
    for copy in copies:
        copy.start()
    for copy in copies:
        copy.wait()


def insert_kernel(own, across, beside, corner, slab_rows, tables, out, rows_all, spectrum):
    side, core = lax.axis_index("xl"), lax.axis_index("co")
    rows_all[side, core] = own[...]
    rows_all[side, 1 - core] = across[...]
    rows_all[1 - side, core] = beside[...]
    rows_all[1 - side, 1 - core] = corner[...]
    for plane in range(8):
        found = jnp.zeros((64, N), F32)
        for o in range(ORIENT):
            rows = slice(64 * (o % 3), 64 * (o % 3) + 64)
            factor = jnp.concatenate([rows_all[o // 3, c, rows, :] for c in range(2)], axis=1)
            found += rows_dot(factor, slab_rows[o, plane])
        start = (plane // 4) * 128 + plane % 4
        for part in range(4):
            rows, lanes = 32 * (part // 2), 128 * (part % 2)
            spectrum[part, pl.ds(start, 32, stride=4), :] = found[
                rows : rows + 32, lanes : lanes + 128
            ]
    lane = lax.broadcasted_iota(jnp.int32, (128, 128), 1)
    both = jnp.concatenate([spectrum[part] for part in range(4)], axis=1).astype(BF16)
    result = plain_dot(both, tables[1]) + plain_dot(both, tables[2])
    for e in range(4):
        early = result[:128, 128 * e : 128 * e + 128]
        late = result[128:, 128 * e : 128 * e + 128]
        even = jnp.where(lane < 64, early, pltpu.roll(late, 64, 1))
        odd = jnp.where(lane < 64, pltpu.roll(early, 64, 1), late)
        out[2 * e] = even.astype(BF16)
        out[2 * e + 1] = odd.astype(BF16)


def last_kernel(pencils, z_high, z_low, out):
    scaling = 1.0 / (N**1.5 * math.sqrt(2048))
    rows = []
    for d in range(8):
        turned = pencils[d].astype(F32).T.astype(BF16)
        rows.append(jnp.concatenate([turned[32 * q : 32 * q + 32] for q in range(4)], axis=1))
    stacked = jnp.concatenate(rows, axis=0)
    result = plain_dot(stacked, z_high[...]) + plain_dot(stacked, z_low[...])
    for d in range(8):
        out[d] = result[32 * d : 32 * d + 32] * scaling


VMEM_SPEC = pl.BlockSpec(memory_space=pltpu.VMEM)
SMEM_SPEC = pl.BlockSpec(memory_space=pltpu.SMEM)
HBM_SPEC = pl.BlockSpec(memory_space=pltpu.HBM)
FRONT_LIMIT = 53500 * 1024
FETCH_LIMIT = 44000 * 1024
INSERT_LIMIT = 44000 * 1024
LAST_LIMIT = 32768 * 1024


def swap(array, bits):
    return lax.ppermute(array, ("xl", "co"), [(i, i ^ bits) for i in range(4)])


def total_of(pieces):
    return jnp.sum(pieces.astype(F32), axis=0).astype(BF16)


def on_device(images, orient_ids, shift_ids, group_ids, translations, defocus, in_plane, slab_rows):
    tables = jnp.asarray(np.stack([x_table()[0], *y_table()]))
    codes = orient_ids + 8 * shift_ids + 128 * group_ids
    scalars = (
        jnp.pad(translations.T, ((0, 0), (0, 16)))
        + jnp.pad(codes.astype(F32)[None], ((0, 1), (16, 8)))
        + jnp.pad(defocus[None], ((0, 1), (24, 0)))
    )
    keep, send = pl.pallas_call(
        front_kernel,
        out_shape=[
            jax.ShapeDtypeStruct((8, 384, 128), BF16),
            jax.ShapeDtypeStruct((8, 384, 128), BF16),
        ],
        in_specs=[SMEM_SPEC] + [HBM_SPEC] * 3,
        out_specs=[VMEM_SPEC] * 2,
        scratch_shapes=[
            pltpu.VMEM((ORIENT, N, 2 * N), F32),
            pltpu.VMEM((IMG, N, 2 * N), BF16),
            pltpu.VMEM((ORIENT, N, N), BF16),
            pltpu.VMEM((512, 512), BF16),
            pltpu.SemaphoreType.DMA((2,)),
            pltpu.SemaphoreType.DMA((IMG,)),
        ],
        compiler_params=pltpu.CompilerParams(vmem_limit_bytes=FRONT_LIMIT),
        name="front",
    )(
        scalars, images, in_plane, tables,
    )
    other = lax.ppermute(send, "co", [(0, 1), (1, 0)])
    pair = (keep.astype(F32) + other.astype(F32)).astype(BF16)
    pieces = lax.all_to_all(
        pair.reshape(16, 192, 128), DOM + ("xl",), split_axis=0, concat_axis=0, tiled=True
    )
    part = total_of(pieces)
    pieces = lax.all_to_all(
        jnp.broadcast_to(part[None], (8, 192, 128)), "zz", split_axis=0, concat_axis=0, tiled=True
    )
    own = total_of(pieces)
    fetched = pl.pallas_call(
        fetch_kernel,
        out_shape=jax.ShapeDtypeStruct(slab_rows.shape, BF16),
        in_specs=[VMEM_SPEC, HBM_SPEC],
        out_specs=VMEM_SPEC,
        scratch_shapes=[pltpu.SemaphoreType.DMA((ORIENT,))],
        compiler_params=pltpu.CompilerParams(vmem_limit_bytes=FETCH_LIMIT),
        cost_estimate=pl.CostEstimate(flops=0, bytes_accessed=12_000_000, transcendentals=0),
        name="fetch",
    )(own, slab_rows)
    sent = pl.pallas_call(
        insert_kernel,
        out_shape=jax.ShapeDtypeStruct((8, 128, 128), BF16),
        in_specs=[VMEM_SPEC] * 6,
        out_specs=VMEM_SPEC,
        scratch_shapes=[
            pltpu.VMEM((2, 2, 192, 128), BF16),
            pltpu.VMEM((4, N, 128), F32),
        ],
        compiler_params=pltpu.CompilerParams(vmem_limit_bytes=INSERT_LIMIT),
        name="insert",
    )(own, swap(own, 1), swap(own, 2), swap(own, 3), fetched, tables)
    pencils = lax.all_to_all(
        sent.reshape(256, 4, 128), ALL, split_axis=0, concat_axis=0, tiled=True
    )
    z_high, z_low = z_table()
    return pl.pallas_call(
        last_kernel,
        out_shape=jax.ShapeDtypeStruct((8, 32, N), F32),
        in_specs=[VMEM_SPEC] * 3,
        out_specs=VMEM_SPEC,
        compiler_params=pltpu.CompilerParams(vmem_limit_bytes=LAST_LIMIT),
        name="last",
    )(pencils.reshape(8, 128, 128), jnp.asarray(z_high), jnp.asarray(z_low))


def solution(mesh):
    fine = Mesh(mesh.devices.reshape(2, 4, 8, 2, 2), ALL)
    return jax.shard_map(
        on_device,
        mesh=fine,
        in_specs=(
            P(ALL, None, None),
            P(ALL),
            P(ALL),
            P(ALL),
            P(),
            P(),
            P(),
            P(None, SLAB, None, None),
        ),
        out_specs=P(SLAB, DOM, None),
        check_vma=False,
    )
```

```python
import math

import jax
import jax.numpy as jnp
import numpy as np
from jax import lax
from jax.experimental import pallas as pl
from jax.experimental.pallas import tpu as pltpu
from jax.sharding import Mesh
from jax.sharding import PartitionSpec as P

N = 256
ORIENT = 6
IMG = 8
WAIT = 4
BF16 = jnp.bfloat16
F32 = jnp.float32

DOM = ("xh", "yy")
SLAB = ("zz", "xl", "co")
ALL = DOM + SLAB


def split_table(table):
    high = table.astype(jnp.bfloat16)
    low = (table - high.astype(np.float64)).astype(jnp.bfloat16)
    return high, low


def phases(left, right):
    angles = (np.outer(left, right) % N) * (2.0 * math.pi / N)
    return np.cos(angles), np.sin(angles)


def x_table():
    x_of = (8 * np.arange(32)[None, :] + np.arange(8)[:, None]).reshape(-1)
    cosine, sine = (t.reshape(8, 32, N) for t in phases(x_of, np.arange(N)))
    real_rows = np.concatenate([cosine, -sine], axis=2)
    imag_rows = np.concatenate([sine, cosine], axis=2)
    return split_table(np.stack([real_rows, imag_rows], axis=1).reshape(512, 512))


def y_table():
    cosine, sine = (t.reshape(N, 8, 32) for t in phases(np.arange(N), np.arange(N)))
    from_real = np.stack([cosine, sine], axis=2).reshape(N, 512)
    from_imag = np.stack([-sine, cosine], axis=2).reshape(N, 512)
    return split_table(np.concatenate([from_real, from_imag], axis=0))


def z_table():
    half, slab, part = np.meshgrid(np.arange(2), np.arange(32), np.arange(4), indexing="ij")
    kz_of = (8 * slab + 4 * half + part).reshape(-1)
    cosine, sine = (t.reshape(2, 128, N) for t in phases(kz_of, np.arange(N)))
    return split_table(np.stack([cosine, -sine], axis=1).reshape(512, N))


def rows_dot(left, right):
    return lax.dot_general(left, right, (((1,), (1,)), ((), ())), preferred_element_type=F32)


def plain_dot(left, right):
    return jnp.dot(left, right, preferred_element_type=F32)


def front_kernel(
    scalars_in, images_hbm, in_plane_hbm, tables,
    keep, send,
    total, images, in_plane, x_rows, scalars, big_sems, image_sems,
):
    scalar_copy = pltpu.make_async_copy(scalars_in, scalars, big_sems.at[2])
    scalar_copy.start()
    image_copies = [
        pltpu.make_async_copy(images_hbm.at[p], images.at[p], image_sems.at[p]) for p in range(IMG)
    ]
    for copy in image_copies:
        copy.start()
    plane_copy = pltpu.make_async_copy(in_plane_hbm, in_plane, big_sems.at[0])
    table_copy = pltpu.make_async_copy(tables.at[0], x_rows, big_sems.at[1])
    total[...] = jnp.zeros_like(total)
    scalar_copy.wait()
    position = lax.broadcasted_iota(jnp.int32, (IMG, N), 1)
    freq = jnp.where(position < N // 2, position, position - N).astype(F32)
    row = lax.broadcasted_iota(jnp.int32, (IMG, N), 0)
    shift_y = jnp.zeros((IMG, N), F32)
    shift_x = jnp.zeros((IMG, N), F32)
    focus = jnp.zeros((IMG, N), F32)
    classes = []
    for p in range(IMG):
        code = scalars[0, 16 + p].astype(jnp.int32)
        shift, group = (code // 8) % 16, code // 128
        classes.append(code % 8)
        shift_y = jnp.where(row == p, scalars[0, shift], shift_y)
        shift_x = jnp.where(row == p, scalars[1, shift], shift_x)
        focus = jnp.where(row == p, scalars[0, 24 + group], focus)
    squares = freq * freq * (1.0 / (N // 2) ** 2)
    step = 2.0 * math.pi / N
    angles = jnp.concatenate(
        [
            step * shift_y * freq,
            focus * squares + 0.1,
            step * shift_x * freq,
            focus * squares,
        ],
        axis=0,
    )
    sines = jnp.sin(angles)
    cosines = jnp.cos(angles)
    columns = jnp.concatenate([sines, cosines, jnp.zeros((64, N), F32)], axis=0).T
    chunk = 32
    for p in range(IMG):
        if p % WAIT == 0:
            for copy in image_copies[p : p + WAIT]:
                copy.wait()
        if p == 0:
            plane_copy.start()
            table_copy.start()
        sin_tx, sin_fx = sines[16 + p : 17 + p], sines[24 + p : 25 + p]
        cos_tx, cos_fx = cosines[16 + p : 17 + p], cosines[24 + p : 25 + p]
        which = classes[p]
        for r in range(0, N, chunk):
            rows = slice(r, r + chunk)
            sin_ty = columns[rows, p : p + 1]
            sin_fy = columns[rows, 8 + p : 9 + p]
            cos_ty = columns[rows, 32 + p : 33 + p]
            cos_fy = columns[rows, 40 + p : 41 + p]
            contrast = -(sin_fy * cos_fx + cos_fy * sin_fx)
            turn_re = contrast * (cos_ty * cos_tx - sin_ty * sin_tx)
            turn_im = contrast * (sin_ty * cos_tx + cos_ty * sin_tx)
            real_part = images[p, rows, :N].astype(F32)
            imag_part = images[p, rows, N:].astype(F32)
            total[which, rows, :N] += real_part * turn_re + imag_part * turn_im
            total[which, rows, N:] += imag_part * turn_re - real_part * turn_im
    first = lax.axis_index("co") == 0
    plane_copy.wait()
    table_copy.wait()
    for o in range(ORIENT):
        sums = total[o].astype(BF16)
        matrix = in_plane[o]
        mixed = jnp.concatenate(
            [plain_dot(sums[:, :N], matrix), plain_dot(sums[:, N:], matrix)], axis=1
        ).astype(BF16)
        along = rows_dot(x_rows[...], mixed).astype(BF16)
        low_half, high_half = along[:, :128], along[:, 128:]
        own = jnp.where(first, low_half, high_half)
        other = jnp.where(first, high_half, low_half)
        rows = slice(64 * (o % 3), 64 * (o % 3) + 64)
        for d in range(8):
            to = 8 * (d // 4) + 4 * (o // 3) + d % 4
            keep[to, rows, :] = own[64 * d : 64 * d + 64]
            send[to, rows, :] = other[64 * d : 64 * d + 64]


def fetch_kernel(after, slab_hbm, slab_rows, sems):
    del after
    copies = [
        pltpu.make_async_copy(slab_hbm.at[o], slab_rows.at[o], sems.at[o]) for o in range(ORIENT)
    ]
    for copy in copies:
        copy.start()
    for copy in copies:
        copy.wait()


def insert_kernel(own, across, beside, corner, slab_rows, tables, out, rows_all, spectrum):
    side, core = lax.axis_index("xl"), lax.axis_index("co")
    rows_all[side, core] = own[...]
    rows_all[side, 1 - core] = across[...]
    rows_all[1 - side, core] = beside[...]
    rows_all[1 - side, 1 - core] = corner[...]
    for plane in range(8):
        found = jnp.zeros((64, N), F32)
        for o in range(ORIENT):
            rows = slice(64 * (o % 3), 64 * (o % 3) + 64)
            factor = jnp.concatenate([rows_all[o // 3, c, rows, :] for c in range(2)], axis=1)
            found += rows_dot(factor, slab_rows[o, plane])
        start = (plane // 4) * 128 + plane % 4
        for part in range(4):
            rows, lanes = 32 * (part // 2), 128 * (part % 2)
            spectrum[part, pl.ds(start, 32, stride=4), :] = found[
                rows : rows + 32, lanes : lanes + 128
            ]
    lane = lax.broadcasted_iota(jnp.int32, (128, 128), 1)
    both = jnp.concatenate([spectrum[part] for part in range(4)], axis=1).astype(BF16)
    result = plain_dot(both, tables[1]) + plain_dot(both, tables[2])
    for e in range(4):
        early = result[:128, 128 * e : 128 * e + 128]
        late = result[128:, 128 * e : 128 * e + 128]
        even = jnp.where(lane < 64, early, pltpu.roll(late, 64, 1))
        odd = jnp.where(lane < 64, pltpu.roll(early, 64, 1), late)
        out[2 * e] = even.astype(BF16)
        out[2 * e + 1] = odd.astype(BF16)


def last_kernel(pencils, z_high, z_low, out):
    scaling = 1.0 / (N**1.5 * math.sqrt(2048))
    rows = []
    for d in range(8):
        turned = pencils[d].astype(F32).T.astype(BF16)
        rows.append(jnp.concatenate([turned[32 * q : 32 * q + 32] for q in range(4)], axis=1))
    stacked = jnp.concatenate(rows, axis=0)
    result = plain_dot(stacked, z_high[...]) + plain_dot(stacked, z_low[...])
    for d in range(8):
        out[d] = result[32 * d : 32 * d + 32] * scaling


VMEM_SPEC = pl.BlockSpec(memory_space=pltpu.VMEM)
HBM_SPEC = pl.BlockSpec(memory_space=pltpu.HBM)
FRONT_LIMIT = 53500 * 1024
FETCH_LIMIT = 44000 * 1024
INSERT_LIMIT = 44000 * 1024
LAST_LIMIT = 32768 * 1024


def swap(array, bits):
    return lax.ppermute(array, ("xl", "co"), [(i, i ^ bits) for i in range(4)])


def total_of(pieces):
    return jnp.sum(pieces.astype(F32), axis=0).astype(BF16)


def on_device(images, orient_ids, shift_ids, group_ids, translations, defocus, in_plane, slab_rows):
    tables = jnp.asarray(np.stack([x_table()[0], *y_table()]))
    spread = ((0, 1), (16, 8))
    scalars = (
        jnp.pad(translations.T, ((0, 0), (0, 16)))
        + jnp.pad(orient_ids[None], spread).astype(F32)
        + jnp.pad(shift_ids[None], spread).astype(F32) * 8.0
        + jnp.pad(group_ids[None], spread).astype(F32) * 128.0
        + jnp.pad(defocus[None], ((0, 1), (24, 0)))
    )
    keep, send = pl.pallas_call(
        front_kernel,
        out_shape=[
            jax.ShapeDtypeStruct((16, 192, 128), BF16),
            jax.ShapeDtypeStruct((16, 192, 128), BF16),
        ],
        in_specs=[HBM_SPEC] * 4,
        out_specs=[VMEM_SPEC] * 2,
        scratch_shapes=[
            pltpu.VMEM((ORIENT, N, 2 * N), F32),
            pltpu.VMEM((IMG, N, 2 * N), BF16),
            pltpu.VMEM((ORIENT, N, N), BF16),
            pltpu.VMEM((512, 512), BF16),
            pltpu.SMEM((2, 32), F32),
            pltpu.SemaphoreType.DMA((3,)),
            pltpu.SemaphoreType.DMA((IMG,)),
        ],
        compiler_params=pltpu.CompilerParams(vmem_limit_bytes=FRONT_LIMIT),
        name="front",
    )(
        scalars, images, in_plane, tables,
    )
    other = lax.ppermute(send, "co", [(0, 1), (1, 0)])
    pair = (keep.astype(F32) + other.astype(F32)).astype(BF16)
    pieces = lax.all_to_all(
        pair, ("xh", "xl", "yy"), split_axis=0, concat_axis=0, tiled=True
    )
    part = total_of(pieces)
    pieces = lax.all_to_all(
        jnp.broadcast_to(part[None], (8, 192, 128)), "zz", split_axis=0, concat_axis=0, tiled=True
    )
    own = total_of(pieces)
    fetched = pl.pallas_call(
        fetch_kernel,
        out_shape=jax.ShapeDtypeStruct(slab_rows.shape, BF16),
        in_specs=[VMEM_SPEC, HBM_SPEC],
        out_specs=VMEM_SPEC,
        scratch_shapes=[pltpu.SemaphoreType.DMA((ORIENT,))],
        compiler_params=pltpu.CompilerParams(vmem_limit_bytes=FETCH_LIMIT),
        cost_estimate=pl.CostEstimate(flops=0, bytes_accessed=12_000_000, transcendentals=0),
        name="fetch",
    )(own, slab_rows)
    sent = pl.pallas_call(
        insert_kernel,
        out_shape=jax.ShapeDtypeStruct((8, 128, 128), BF16),
        in_specs=[VMEM_SPEC] * 6,
        out_specs=VMEM_SPEC,
        scratch_shapes=[
            pltpu.VMEM((2, 2, 192, 128), BF16),
            pltpu.VMEM((4, N, 128), F32),
        ],
        compiler_params=pltpu.CompilerParams(vmem_limit_bytes=INSERT_LIMIT),
        name="insert",
    )(own, swap(own, 1), swap(own, 2), swap(own, 3), fetched, tables)
    pencils = lax.all_to_all(
        sent.reshape(256, 4, 128), ALL, split_axis=0, concat_axis=0, tiled=True
    )
    z_high, z_low = z_table()
    return pl.pallas_call(
        last_kernel,
        out_shape=jax.ShapeDtypeStruct((8, 32, N), F32),
        in_specs=[VMEM_SPEC] * 3,
        out_specs=VMEM_SPEC,
        compiler_params=pltpu.CompilerParams(vmem_limit_bytes=LAST_LIMIT),
        name="last",
    )(pencils.reshape(8, 128, 128), jnp.asarray(z_high), jnp.asarray(z_low))


def solution(mesh):
    fine = Mesh(mesh.devices.reshape(2, 4, 8, 2, 2), ALL)
    return jax.shard_map(
        on_device,
        mesh=fine,
        in_specs=(
            P(ALL, None, None),
            P(ALL),
            P(ALL),
            P(ALL),
            P(),
            P(),
            P(),
            P(None, SLAB, None, None),
        ),
        out_specs=P(SLAB, DOM, None),
        check_vma=False,
    )
```

```python
import math

import jax
import jax.numpy as jnp
import numpy as np
from jax import lax
from jax.experimental import pallas as pl
from jax.experimental.pallas import tpu as pltpu
from jax.sharding import Mesh
from jax.sharding import PartitionSpec as P

N = 256
ORIENT = 6
IMG = 8
WAIT = 4
BF16 = jnp.bfloat16
F32 = jnp.float32

DOM = ("xh", "yy")
SLAB = ("zz", "xl", "co")
ALL = DOM + SLAB


def split_table(table):
    high = table.astype(jnp.bfloat16)
    low = (table - high.astype(np.float64)).astype(jnp.bfloat16)
    return high, low


def phases(left, right):
    angles = (np.outer(left, right) % N) * (2.0 * math.pi / N)
    return np.cos(angles), np.sin(angles)


def x_table():
    x_of = (8 * np.arange(31, -1, -1)[None, :] + np.arange(8)[:, None]).reshape(-1)
    cosine, sine = (t.reshape(8, 32, N) for t in phases(x_of, np.arange(N)))
    real_rows = np.concatenate([cosine, -sine], axis=2)
    imag_rows = np.concatenate([sine, cosine], axis=2)
    return split_table(np.stack([real_rows, imag_rows], axis=1).reshape(512, 512))


def y_table():
    cosine, sine = (t.reshape(N, 8, 32) for t in phases(np.arange(N), np.arange(N)))
    from_real = np.stack([cosine, sine], axis=2).reshape(N, 512)
    from_imag = np.stack([-sine, cosine], axis=2).reshape(N, 512)
    return split_table(np.concatenate([from_real, from_imag], axis=0))


def z_table():
    half, slab, part = np.meshgrid(np.arange(2), np.arange(31, -1, -1), np.arange(4), indexing="ij")
    kz_of = (8 * slab + 4 * half + part).reshape(-1)
    cosine, sine = (t.reshape(2, 128, N) for t in phases(kz_of, np.arange(N)))
    return split_table(np.stack([cosine, -sine], axis=1).reshape(512, N))


def rows_dot(left, right):
    return lax.dot_general(left, right, (((1,), (1,)), ((), ())), preferred_element_type=F32)


def plain_dot(left, right):
    return jnp.dot(left, right, preferred_element_type=F32)


def front_kernel(
    scalars_in, images_hbm, in_plane_hbm, tables,
    keep, send,
    total, images, in_plane, x_rows, scalars, big_sems, image_sems,
):
    scalar_copy = pltpu.make_async_copy(scalars_in, scalars, big_sems.at[2])
    scalar_copy.start()
    image_copies = [
        pltpu.make_async_copy(images_hbm.at[p], images.at[p], image_sems.at[p]) for p in range(IMG)
    ]
    for copy in image_copies:
        copy.start()
    plane_copy = pltpu.make_async_copy(in_plane_hbm, in_plane, big_sems.at[0])
    table_copy = pltpu.make_async_copy(tables.at[0], x_rows, big_sems.at[1])
    total[...] = jnp.zeros_like(total)
    scalar_copy.wait()
    position = lax.broadcasted_iota(jnp.int32, (IMG, N), 1)
    freq = jnp.where(position < N // 2, position, position - N).astype(F32)
    row = lax.broadcasted_iota(jnp.int32, (IMG, N), 0)
    shift_y = jnp.zeros((IMG, N), F32)
    shift_x = jnp.zeros((IMG, N), F32)
    focus = jnp.zeros((IMG, N), F32)
    classes = []
    for p in range(IMG):
        code = scalars[0, 16 + p].astype(jnp.int32)
        shift, group = (code // 8) % 16, code // 128
        classes.append(code % 8)
        shift_y = jnp.where(row == p, scalars[0, shift], shift_y)
        shift_x = jnp.where(row == p, scalars[1, shift], shift_x)
        focus = jnp.where(row == p, scalars[0, 24 + group], focus)
    squares = freq * freq * (1.0 / (N // 2) ** 2)
    step = 2.0 * math.pi / N
    angles = jnp.concatenate(
        [
            step * shift_y * freq,
            focus * squares + 0.1,
            step * shift_x * freq,
            focus * squares,
        ],
        axis=0,
    )
    sines = jnp.sin(angles)
    cosines = jnp.cos(angles)
    columns = jnp.concatenate([sines, cosines, jnp.zeros((64, N), F32)], axis=0).T
    chunk = 32
    for p in range(IMG):
        if p % WAIT == 0:
            for copy in image_copies[p : p + WAIT]:
                copy.wait()
        if p == 0:
            plane_copy.start()
            table_copy.start()
        sin_tx, sin_fx = sines[16 + p : 17 + p], sines[24 + p : 25 + p]
        cos_tx, cos_fx = cosines[16 + p : 17 + p], cosines[24 + p : 25 + p]
        which = classes[p]
        for r in range(0, N, chunk):
            rows = slice(r, r + chunk)
            sin_ty = columns[rows, p : p + 1]
            sin_fy = columns[rows, 8 + p : 9 + p]
            cos_ty = columns[rows, 32 + p : 33 + p]
            cos_fy = columns[rows, 40 + p : 41 + p]
            contrast = -(sin_fy * cos_fx + cos_fy * sin_fx)
            turn_re = contrast * (cos_ty * cos_tx - sin_ty * sin_tx)
            turn_im = contrast * (sin_ty * cos_tx + cos_ty * sin_tx)
            real_part = images[p, rows, :N].astype(F32)
            imag_part = images[p, rows, N:].astype(F32)
            total[which, rows, :N] += real_part * turn_re + imag_part * turn_im
            total[which, rows, N:] += imag_part * turn_re - real_part * turn_im
    first = lax.axis_index("co") == 0
    plane_copy.wait()
    table_copy.wait()
    for o in range(ORIENT):
        sums = total[o].astype(BF16)
        matrix = in_plane[o]
        mixed = jnp.concatenate(
            [plain_dot(sums[:, :N], matrix), plain_dot(sums[:, N:], matrix)], axis=1
        ).astype(BF16)
        along = rows_dot(x_rows[...], mixed).astype(BF16)
        low_half, high_half = along[:, :128], along[:, 128:]
        own = jnp.where(first, low_half, high_half)
        other = jnp.where(first, high_half, low_half)
        rows = slice(64 * (o % 3), 64 * (o % 3) + 64)
        for d in range(8):
            to = 15 - (8 * (d // 4) + 4 * (o // 3) + d % 4)
            keep[to, rows, :] = own[64 * d : 64 * d + 64]
            send[to, rows, :] = other[64 * d : 64 * d + 64]


def fetch_kernel(after, slab_hbm, slab_rows, sems):
    del after
    copies = [
        pltpu.make_async_copy(slab_hbm.at[o], slab_rows.at[o], sems.at[o]) for o in range(ORIENT)
    ]
    for copy in copies:
        copy.start()
    for copy in copies:
        copy.wait()


def insert_kernel(own, across, beside, corner, slab_rows, tables, out, rows_all, spectrum):
    side, core = lax.axis_index("xl"), lax.axis_index("co")
    rows_all[side, core] = own[...]
    rows_all[side, 1 - core] = across[...]
    rows_all[1 - side, core] = beside[...]
    rows_all[1 - side, 1 - core] = corner[...]
    for plane in range(8):
        found = jnp.zeros((64, N), F32)
        for o in range(ORIENT):
            rows = slice(64 * (o % 3), 64 * (o % 3) + 64)
            factor = jnp.concatenate([rows_all[o // 3, c, rows, :] for c in range(2)], axis=1)
            found += rows_dot(factor, slab_rows[o, plane])
        start = (plane // 4) * 128 + plane % 4
        for part in range(4):
            rows, lanes = 32 * (part // 2), 128 * (part % 2)
            spectrum[part, pl.ds(start, 32, stride=4), :] = found[
                rows : rows + 32, lanes : lanes + 128
            ]
    lane = lax.broadcasted_iota(jnp.int32, (128, 128), 1)
    both = jnp.concatenate([spectrum[part] for part in range(4)], axis=1).astype(BF16)
    result = plain_dot(both, tables[1]) + plain_dot(both, tables[2])
    for e in range(4):
        early = result[:128, 128 * e : 128 * e + 128]
        late = result[128:, 128 * e : 128 * e + 128]
        even = jnp.where(lane < 64, early, pltpu.roll(late, 64, 1))
        odd = jnp.where(lane < 64, pltpu.roll(early, 64, 1), late)
        out[7 - 2 * e] = even.astype(BF16)
        out[6 - 2 * e] = odd.astype(BF16)


def last_kernel(pencils, z_high, z_low, out):
    scaling = 1.0 / (N**1.5 * math.sqrt(2048))
    rows = []
    for d in range(8):
        turned = pencils[d].astype(F32).T.astype(BF16)
        rows.append(jnp.concatenate([turned[32 * q : 32 * q + 32] for q in range(4)], axis=1))
    stacked = jnp.concatenate(rows, axis=0)
    result = plain_dot(stacked, z_high[...]) + plain_dot(stacked, z_low[...])
    for d in range(8):
        out[7 - d] = result[32 * d : 32 * d + 32] * scaling


VMEM_SPEC = pl.BlockSpec(memory_space=pltpu.VMEM)
HBM_SPEC = pl.BlockSpec(memory_space=pltpu.HBM)
FRONT_LIMIT = 53500 * 1024
FETCH_LIMIT = 44000 * 1024
INSERT_LIMIT = 44000 * 1024
LAST_LIMIT = 32768 * 1024


def swap(array, bits):
    return lax.ppermute(array, ("xl", "co"), [(i, i ^ bits) for i in range(4)])


def exchange(array, axes):
    count = array.shape[0]
    return lax.all_to_all(
        array,
        axes,
        split_axis=0,
        concat_axis=0,
        tiled=True,
        axis_index_groups=[list(range(count - 1, -1, -1))],
    )


def total_of(pieces):
    return jnp.sum(pieces.astype(F32), axis=0).astype(BF16)


def on_device(images, orient_ids, shift_ids, group_ids, translations, defocus, in_plane, slab_rows):
    tables = jnp.asarray(np.stack([x_table()[0], *y_table()]))
    spread = ((0, 1), (16, 8))
    scalars = (
        jnp.pad(translations.T, ((0, 0), (0, 16)))
        + jnp.pad(orient_ids[None], spread).astype(F32)
        + jnp.pad(shift_ids[None], spread).astype(F32) * 8.0
        + jnp.pad(group_ids[None], spread).astype(F32) * 128.0
        + jnp.pad(defocus[None], ((0, 1), (24, 0)))
    )
    keep, send = pl.pallas_call(
        front_kernel,
        out_shape=[
            jax.ShapeDtypeStruct((16, 192, 128), BF16),
            jax.ShapeDtypeStruct((16, 192, 128), BF16),
        ],
        in_specs=[HBM_SPEC] * 4,
        out_specs=[VMEM_SPEC] * 2,
        scratch_shapes=[
            pltpu.VMEM((ORIENT, N, 2 * N), F32),
            pltpu.VMEM((IMG, N, 2 * N), BF16),
            pltpu.VMEM((ORIENT, N, N), BF16),
            pltpu.VMEM((512, 512), BF16),
            pltpu.SMEM((2, 32), F32),
            pltpu.SemaphoreType.DMA((3,)),
            pltpu.SemaphoreType.DMA((IMG,)),
        ],
        compiler_params=pltpu.CompilerParams(vmem_limit_bytes=FRONT_LIMIT),
        name="front",
    )(
        scalars, images, in_plane, tables,
    )
    other = lax.ppermute(send, "co", [(0, 1), (1, 0)])
    pair = (keep.astype(F32) + other.astype(F32)).astype(BF16)
    pieces = exchange(pair, ("xh", "xl", "yy"))
    part = total_of(pieces)
    pieces = exchange(jnp.broadcast_to(part[None], (8, 192, 128)), "zz")
    own = total_of(pieces)
    fetched = pl.pallas_call(
        fetch_kernel,
        out_shape=jax.ShapeDtypeStruct(slab_rows.shape, BF16),
        in_specs=[VMEM_SPEC, HBM_SPEC],
        out_specs=VMEM_SPEC,
        scratch_shapes=[pltpu.SemaphoreType.DMA((ORIENT,))],
        compiler_params=pltpu.CompilerParams(vmem_limit_bytes=FETCH_LIMIT),
        cost_estimate=pl.CostEstimate(flops=0, bytes_accessed=12_000_000, transcendentals=0),
        name="fetch",
    )(own, slab_rows)
    sent = pl.pallas_call(
        insert_kernel,
        out_shape=jax.ShapeDtypeStruct((8, 128, 128), BF16),
        in_specs=[VMEM_SPEC] * 6,
        out_specs=VMEM_SPEC,
        scratch_shapes=[
            pltpu.VMEM((2, 2, 192, 128), BF16),
            pltpu.VMEM((4, N, 128), F32),
        ],
        compiler_params=pltpu.CompilerParams(vmem_limit_bytes=INSERT_LIMIT),
        name="insert",
    )(own, swap(own, 1), swap(own, 2), swap(own, 3), fetched, tables)
    pencils = exchange(sent.reshape(256, 4, 128), ALL)
    z_high, z_low = z_table()
    return pl.pallas_call(
        last_kernel,
        out_shape=jax.ShapeDtypeStruct((8, 32, N), F32),
        in_specs=[VMEM_SPEC] * 3,
        out_specs=VMEM_SPEC,
        compiler_params=pltpu.CompilerParams(vmem_limit_bytes=LAST_LIMIT),
        name="last",
    )(pencils.reshape(8, 128, 128), jnp.asarray(z_high), jnp.asarray(z_low))


def solution(mesh):
    fine = Mesh(mesh.devices.reshape(2, 4, 8, 2, 2), ALL)
    return jax.shard_map(
        on_device,
        mesh=fine,
        in_specs=(
            P(ALL, None, None),
            P(ALL),
            P(ALL),
            P(ALL),
            P(),
            P(),
            P(),
            P(None, SLAB, None, None),
        ),
        out_specs=P(SLAB, DOM, None),
        check_vma=False,
    )
```

```python
import math

import jax
import jax.numpy as jnp
import numpy as np
from jax import lax
from jax.experimental import pallas as pl
from jax.experimental.pallas import tpu as pltpu
from jax.sharding import Mesh
from jax.sharding import PartitionSpec as P

N = 256
ORIENT = 6
IMG = 8
WAIT = 4
EARLY = 3
BF16 = jnp.bfloat16
F32 = jnp.float32

DOM = ("xh", "yy")
SLAB = ("zz", "xl", "co")
ALL = DOM + SLAB


def split_table(table):
    high = table.astype(jnp.bfloat16)
    low = (table - high.astype(np.float64)).astype(jnp.bfloat16)
    return high, low


def phases(left, right):
    angles = (np.outer(left, right) % N) * (2.0 * math.pi / N)
    return np.cos(angles), np.sin(angles)


def x_table():
    x_of = (8 * np.arange(31, -1, -1)[None, :] + np.arange(8)[:, None]).reshape(-1)
    cosine, sine = (t.reshape(8, 32, N) for t in phases(x_of, np.arange(N)))
    real_rows = np.concatenate([cosine, -sine], axis=2)
    imag_rows = np.concatenate([sine, cosine], axis=2)
    return split_table(np.stack([real_rows, imag_rows], axis=1).reshape(512, 512))


def y_table():
    cosine, sine = (t.reshape(N, 8, 32) for t in phases(np.arange(N), np.arange(N)))
    from_real = np.stack([cosine, sine], axis=2).reshape(N, 512)
    from_imag = np.stack([-sine, cosine], axis=2).reshape(N, 512)
    return split_table(np.concatenate([from_real, from_imag], axis=0))


def z_table():
    half, slab, part = np.meshgrid(np.arange(2), np.arange(31, -1, -1), np.arange(4), indexing="ij")
    kz_of = (8 * slab + 4 * half + part).reshape(-1)
    cosine, sine = (t.reshape(2, 128, N) for t in phases(kz_of, np.arange(N)))
    return split_table(np.stack([cosine, -sine], axis=1).reshape(512, N))


def rows_dot(left, right):
    return lax.dot_general(left, right, (((1,), (1,)), ((), ())), preferred_element_type=F32)


def plain_dot(left, right):
    return jnp.dot(left, right, preferred_element_type=F32)


def front_kernel(
    scalars_in, images_hbm, in_plane_hbm, tables,
    keep, send,
    total, images, in_plane, x_rows, scalars, big_sems, image_sems,
):
    scalar_copy = pltpu.make_async_copy(scalars_in, scalars, big_sems.at[2])
    scalar_copy.start()
    image_copies = [
        pltpu.make_async_copy(images_hbm.at[p], images.at[p], image_sems.at[p]) for p in range(IMG)
    ]
    for copy in image_copies:
        copy.start()
    plane_copy = pltpu.make_async_copy(in_plane_hbm, in_plane, big_sems.at[0])
    table_copy = pltpu.make_async_copy(tables.at[0], x_rows, big_sems.at[1])
    total[...] = jnp.zeros_like(total)
    scalar_copy.wait()
    position = lax.broadcasted_iota(jnp.int32, (IMG, N), 1)
    freq = jnp.where(position < N // 2, position, position - N).astype(F32)
    row = lax.broadcasted_iota(jnp.int32, (IMG, N), 0)
    shift_y = jnp.zeros((IMG, N), F32)
    shift_x = jnp.zeros((IMG, N), F32)
    focus = jnp.zeros((IMG, N), F32)
    classes = []
    for p in range(IMG):
        code = scalars[0, 16 + p].astype(jnp.int32)
        shift, group = (code // 8) % 16, code // 128
        classes.append(code % 8)
        shift_y = jnp.where(row == p, scalars[0, shift], shift_y)
        shift_x = jnp.where(row == p, scalars[1, shift], shift_x)
        focus = jnp.where(row == p, scalars[0, 24 + group], focus)
    squares = freq * freq * (1.0 / (N // 2) ** 2)
    step = 2.0 * math.pi / N
    angles = jnp.concatenate(
        [
            step * shift_y * freq,
            focus * squares + 0.1,
            step * shift_x * freq,
            focus * squares,
        ],
        axis=0,
    )
    sines = jnp.sin(angles)
    cosines = jnp.cos(angles)
    columns = jnp.concatenate([sines, cosines, jnp.zeros((64, N), F32)], axis=0).T
    chunk = 32
    for p in range(IMG):
        if p % WAIT == 0:
            for copy in image_copies[p : p + WAIT]:
                copy.wait()
        if p == 0:
            plane_copy.start()
            table_copy.start()
        sin_tx, sin_fx = sines[16 + p : 17 + p], sines[24 + p : 25 + p]
        cos_tx, cos_fx = cosines[16 + p : 17 + p], cosines[24 + p : 25 + p]
        which = classes[p]
        for r in range(0, N, chunk):
            rows = slice(r, r + chunk)
            sin_ty = columns[rows, p : p + 1]
            sin_fy = columns[rows, 8 + p : 9 + p]
            cos_ty = columns[rows, 32 + p : 33 + p]
            cos_fy = columns[rows, 40 + p : 41 + p]
            contrast = -(sin_fy * cos_fx + cos_fy * sin_fx)
            turn_re = contrast * (cos_ty * cos_tx - sin_ty * sin_tx)
            turn_im = contrast * (sin_ty * cos_tx + cos_ty * sin_tx)
            real_part = images[p, rows, :N].astype(F32)
            imag_part = images[p, rows, N:].astype(F32)
            total[which, rows, :N] += real_part * turn_re + imag_part * turn_im
            total[which, rows, N:] += imag_part * turn_re - real_part * turn_im
    first = lax.axis_index("co") == 0
    plane_copy.wait()
    table_copy.wait()
    for o in range(ORIENT):
        sums = total[o].astype(BF16)
        matrix = in_plane[o]
        mixed = jnp.concatenate(
            [plain_dot(sums[:, :N], matrix), plain_dot(sums[:, N:], matrix)], axis=1
        ).astype(BF16)
        along = rows_dot(x_rows[...], mixed).astype(BF16)
        low_half, high_half = along[:, :128], along[:, 128:]
        own = jnp.where(first, low_half, high_half)
        other = jnp.where(first, high_half, low_half)
        rows = slice(64 * (o % 3), 64 * (o % 3) + 64)
        for d in range(8):
            to = 15 - (8 * (d // 4) + 4 * (o // 3) + d % 4)
            keep[to, rows, :] = own[64 * d : 64 * d + 64]
            send[to, rows, :] = other[64 * d : 64 * d + 64]


def fetch_kernel(after, slab_hbm, slab_rows, sems):
    del after
    copies = [
        pltpu.make_async_copy(slab_hbm.at[o], slab_rows.at[o], sems.at[o]) for o in range(EARLY)
    ]
    for copy in copies:
        copy.start()
    for copy in copies:
        copy.wait()


def insert_kernel(
    own, across, beside, corner, early_rows, slab_hbm, tables, out,
    rows_all, spectrum, partial, late_rows, sems,
):
    copies = [
        pltpu.make_async_copy(slab_hbm.at[o], late_rows.at[o - EARLY], sems.at[o - EARLY])
        for o in range(EARLY, ORIENT)
    ]
    for copy in copies:
        copy.start()
    side, core = lax.axis_index("xl"), lax.axis_index("co")
    rows_all[side, core] = own[...]
    rows_all[side, 1 - core] = across[...]
    rows_all[1 - side, core] = beside[...]
    rows_all[1 - side, 1 - core] = corner[...]
    factors = [
        jnp.concatenate(
            [rows_all[o // 3, c, 64 * (o % 3) : 64 * (o % 3) + 64, :] for c in range(2)], axis=1
        )
        for o in range(ORIENT)
    ]
    for plane in range(8):
        found = jnp.zeros((64, N), F32)
        for o in range(EARLY):
            found += rows_dot(factors[o], early_rows[o, plane])
        partial[plane] = found
    for copy in copies:
        copy.wait()
    for plane in range(8):
        found = partial[plane]
        for o in range(EARLY, ORIENT):
            found += rows_dot(factors[o], late_rows[o - EARLY, plane])
        start = (plane // 4) * 128 + plane % 4
        for part in range(4):
            rows, lanes = 32 * (part // 2), 128 * (part % 2)
            spectrum[part, pl.ds(start, 32, stride=4), :] = found[
                rows : rows + 32, lanes : lanes + 128
            ]
    lane = lax.broadcasted_iota(jnp.int32, (128, 128), 1)
    both = jnp.concatenate([spectrum[part] for part in range(4)], axis=1).astype(BF16)
    result = plain_dot(both, tables[1]) + plain_dot(both, tables[2])
    for e in range(4):
        early = result[:128, 128 * e : 128 * e + 128]
        late = result[128:, 128 * e : 128 * e + 128]
        even = jnp.where(lane < 64, early, pltpu.roll(late, 64, 1))
        odd = jnp.where(lane < 64, pltpu.roll(early, 64, 1), late)
        out[7 - 2 * e] = even.astype(BF16)
        out[6 - 2 * e] = odd.astype(BF16)


def last_kernel(pencils, z_high, z_low, out):
    scaling = 1.0 / (N**1.5 * math.sqrt(2048))
    rows = []
    for d in range(8):
        turned = pencils[d].astype(F32).T.astype(BF16)
        rows.append(jnp.concatenate([turned[32 * q : 32 * q + 32] for q in range(4)], axis=1))
    stacked = jnp.concatenate(rows, axis=0)
    result = plain_dot(stacked, z_high[...]) + plain_dot(stacked, z_low[...])
    for d in range(8):
        out[7 - d] = result[32 * d : 32 * d + 32] * scaling


VMEM_SPEC = pl.BlockSpec(memory_space=pltpu.VMEM)
HBM_SPEC = pl.BlockSpec(memory_space=pltpu.HBM)
FRONT_LIMIT = 53500 * 1024
FETCH_LIMIT = 49500 * 1024
INSERT_LIMIT = 48000 * 1024
LAST_LIMIT = 32768 * 1024


def swap(array, bits):
    return lax.ppermute(array, ("xl", "co"), [(i, i ^ bits) for i in range(4)])


def exchange(array, axes):
    count = array.shape[0]
    return lax.all_to_all(
        array,
        axes,
        split_axis=0,
        concat_axis=0,
        tiled=True,
        axis_index_groups=[list(range(count - 1, -1, -1))],
    )


def total_of(pieces):
    return jnp.sum(pieces.astype(F32), axis=0).astype(BF16)


def on_device(images, orient_ids, shift_ids, group_ids, translations, defocus, in_plane, slab_rows):
    tables = jnp.asarray(np.stack([x_table()[0], *y_table()]))
    spread = ((0, 1), (16, 8))
    scalars = (
        jnp.pad(translations.T, ((0, 0), (0, 16)))
        + jnp.pad(orient_ids[None], spread).astype(F32)
        + jnp.pad(shift_ids[None], spread).astype(F32) * 8.0
        + jnp.pad(group_ids[None], spread).astype(F32) * 128.0
        + jnp.pad(defocus[None], ((0, 1), (24, 0)))
    )
    keep, send = pl.pallas_call(
        front_kernel,
        out_shape=[
            jax.ShapeDtypeStruct((16, 192, 128), BF16),
            jax.ShapeDtypeStruct((16, 192, 128), BF16),
        ],
        in_specs=[HBM_SPEC] * 4,
        out_specs=[VMEM_SPEC] * 2,
        scratch_shapes=[
            pltpu.VMEM((ORIENT, N, 2 * N), F32),
            pltpu.VMEM((IMG, N, 2 * N), BF16),
            pltpu.VMEM((ORIENT, N, N), BF16),
            pltpu.VMEM((512, 512), BF16),
            pltpu.SMEM((2, 32), F32),
            pltpu.SemaphoreType.DMA((3,)),
            pltpu.SemaphoreType.DMA((IMG,)),
        ],
        compiler_params=pltpu.CompilerParams(vmem_limit_bytes=FRONT_LIMIT),
        name="front",
    )(
        scalars, images, in_plane, tables,
    )
    other = lax.ppermute(send, "co", [(0, 1), (1, 0)])
    pair = (keep.astype(F32) + other.astype(F32)).astype(BF16)
    pieces = exchange(pair, ("xh", "xl", "yy"))
    part = total_of(pieces)
    pieces = exchange(jnp.broadcast_to(part[None], (8, 192, 128)), "zz")
    own = total_of(pieces)
    fetched = pl.pallas_call(
        fetch_kernel,
        out_shape=jax.ShapeDtypeStruct((EARLY, 8, N, N), BF16),
        in_specs=[VMEM_SPEC, HBM_SPEC],
        out_specs=VMEM_SPEC,
        scratch_shapes=[pltpu.SemaphoreType.DMA((EARLY,))],
        compiler_params=pltpu.CompilerParams(vmem_limit_bytes=FETCH_LIMIT),
        cost_estimate=pl.CostEstimate(flops=0, bytes_accessed=6_000_000, transcendentals=0),
        name="fetch",
    )(own, slab_rows)
    sent = pl.pallas_call(
        insert_kernel,
        out_shape=jax.ShapeDtypeStruct((8, 128, 128), BF16),
        in_specs=[VMEM_SPEC] * 5 + [HBM_SPEC, VMEM_SPEC],
        out_specs=VMEM_SPEC,
        scratch_shapes=[
            pltpu.VMEM((2, 2, 192, 128), BF16),
            pltpu.VMEM((4, N, 128), F32),
            pltpu.VMEM((8, 64, N), F32),
            pltpu.VMEM((ORIENT - EARLY, 8, N, N), BF16),
            pltpu.SemaphoreType.DMA((ORIENT - EARLY,)),
        ],
        compiler_params=pltpu.CompilerParams(vmem_limit_bytes=INSERT_LIMIT),
        name="insert",
    )(own, swap(own, 1), swap(own, 2), swap(own, 3), fetched, slab_rows, tables)
    pencils = exchange(sent.reshape(256, 4, 128), ALL)
    z_high, z_low = z_table()
    return pl.pallas_call(
        last_kernel,
        out_shape=jax.ShapeDtypeStruct((8, 32, N), F32),
        in_specs=[VMEM_SPEC] * 3,
        out_specs=VMEM_SPEC,
        compiler_params=pltpu.CompilerParams(vmem_limit_bytes=LAST_LIMIT),
        name="last",
    )(pencils.reshape(8, 128, 128), jnp.asarray(z_high), jnp.asarray(z_low))


def solution(mesh):
    fine = Mesh(mesh.devices.reshape(2, 4, 8, 2, 2), ALL)
    return jax.shard_map(
        on_device,
        mesh=fine,
        in_specs=(
            P(ALL, None, None),
            P(ALL),
            P(ALL),
            P(ALL),
            P(),
            P(),
            P(),
            P(None, SLAB, None, None),
        ),
        out_specs=P(SLAB, DOM, None),
        check_vma=False,
    )
```

```python
import functools
import math

import jax
import jax.numpy as jnp
import numpy as np
from jax import lax
from jax.experimental import pallas as pl
from jax.experimental.pallas import tpu as pltpu
from jax.sharding import Mesh
from jax.sharding import PartitionSpec as P

N = 256
ORIENT = 6
IMG = 8
WAIT = 4
EARLY = 2
BF16 = jnp.bfloat16
F32 = jnp.float32

DOM = ("xh", "yy")
SLAB = ("zz", "xl", "co")
ALL = DOM + SLAB


def split_table(table):
    high = table.astype(jnp.bfloat16)
    low = (table - high.astype(np.float64)).astype(jnp.bfloat16)
    return high, low


def phases(left, right):
    angles = (np.outer(left, right) % N) * (2.0 * math.pi / N)
    return np.cos(angles), np.sin(angles)


def x_table():
    x_of = (8 * np.arange(31, -1, -1)[None, :] + np.arange(8)[:, None]).reshape(-1)
    cosine, sine = (t.reshape(8, 32, N) for t in phases(x_of, np.arange(N)))
    real_rows = np.concatenate([cosine, -sine], axis=2)
    imag_rows = np.concatenate([sine, cosine], axis=2)
    return split_table(np.stack([real_rows, imag_rows], axis=1).reshape(512, 512))


def y_table():
    cosine, sine = (t.reshape(N, 8, 32) for t in phases(np.arange(N), np.arange(N)))
    from_real = np.stack([cosine, sine], axis=2).reshape(N, 512)
    from_imag = np.stack([-sine, cosine], axis=2).reshape(N, 512)
    return split_table(np.concatenate([from_real, from_imag], axis=0))


def z_table():
    half, slab, part = np.meshgrid(np.arange(2), np.arange(31, -1, -1), np.arange(4), indexing="ij")
    kz_of = (8 * slab + 4 * half + part).reshape(-1)
    cosine, sine = (t.reshape(2, 128, N) for t in phases(kz_of, np.arange(N)))
    return split_table(np.stack([cosine, -sine], axis=1).reshape(512, N))


def rows_dot(left, right):
    return lax.dot_general(left, right, (((1,), (1,)), ((), ())), preferred_element_type=F32)


def plain_dot(left, right):
    return jnp.dot(left, right, preferred_element_type=F32)


def front_kernel(
    scalars_in, images_hbm, in_plane_hbm, tables,
    keep, send,
    total, images, in_plane, x_rows, scalars, big_sems, image_sems,
):
    scalar_copy = pltpu.make_async_copy(scalars_in, scalars, big_sems.at[2])
    scalar_copy.start()
    image_copies = [
        pltpu.make_async_copy(images_hbm.at[p], images.at[p], image_sems.at[p]) for p in range(IMG)
    ]
    for copy in image_copies:
        copy.start()
    plane_copy = pltpu.make_async_copy(in_plane_hbm, in_plane, big_sems.at[0])
    table_copy = pltpu.make_async_copy(tables.at[0], x_rows, big_sems.at[1])
    total[...] = jnp.zeros_like(total)
    scalar_copy.wait()
    position = lax.broadcasted_iota(jnp.int32, (IMG, N), 1)
    freq = jnp.where(position < N // 2, position, position - N).astype(F32)
    row = lax.broadcasted_iota(jnp.int32, (IMG, N), 0)
    shift_y = jnp.zeros((IMG, N), F32)
    shift_x = jnp.zeros((IMG, N), F32)
    focus = jnp.zeros((IMG, N), F32)
    classes = []
    for p in range(IMG):
        code = scalars[0, 16 + p].astype(jnp.int32)
        shift, group = (code // 8) % 16, code // 128
        classes.append(code % 8)
        shift_y = jnp.where(row == p, scalars[0, shift], shift_y)
        shift_x = jnp.where(row == p, scalars[1, shift], shift_x)
        focus = jnp.where(row == p, scalars[0, 24 + group], focus)
    squares = freq * freq * (1.0 / (N // 2) ** 2)
    step = 2.0 * math.pi / N
    angles = jnp.concatenate(
        [
            step * shift_y * freq,
            focus * squares + 0.1,
            step * shift_x * freq,
            focus * squares,
        ],
        axis=0,
    )
    sines = jnp.sin(angles)
    cosines = jnp.cos(angles)
    columns = jnp.concatenate([sines, cosines, jnp.zeros((64, N), F32)], axis=0).T
    chunk = 32
    for p in range(IMG):
        if p % WAIT == 0:
            for copy in image_copies[p : p + WAIT]:
                copy.wait()
        if p == 0:
            plane_copy.start()
            table_copy.start()
        sin_tx, sin_fx = sines[16 + p : 17 + p], sines[24 + p : 25 + p]
        cos_tx, cos_fx = cosines[16 + p : 17 + p], cosines[24 + p : 25 + p]
        which = classes[p]
        for r in range(0, N, chunk):
            rows = slice(r, r + chunk)
            sin_ty = columns[rows, p : p + 1]
            sin_fy = columns[rows, 8 + p : 9 + p]
            cos_ty = columns[rows, 32 + p : 33 + p]
            cos_fy = columns[rows, 40 + p : 41 + p]
            contrast = -(sin_fy * cos_fx + cos_fy * sin_fx)
            turn_re = contrast * (cos_ty * cos_tx - sin_ty * sin_tx)
            turn_im = contrast * (sin_ty * cos_tx + cos_ty * sin_tx)
            real_part = images[p, rows, :N].astype(F32)
            imag_part = images[p, rows, N:].astype(F32)
            total[which, rows, :N] += real_part * turn_re + imag_part * turn_im
            total[which, rows, N:] += imag_part * turn_re - real_part * turn_im
    first = lax.axis_index("co") == 0
    plane_copy.wait()
    table_copy.wait()
    for o in range(ORIENT):
        sums = total[o].astype(BF16)
        matrix = in_plane[o]
        mixed = jnp.concatenate(
            [plain_dot(sums[:, :N], matrix), plain_dot(sums[:, N:], matrix)], axis=1
        ).astype(BF16)
        along = rows_dot(x_rows[...], mixed).astype(BF16)
        low_half, high_half = along[:, :128], along[:, 128:]
        own = jnp.where(first, low_half, high_half)
        other = jnp.where(first, high_half, low_half)
        rows = slice(64 * (o % 3), 64 * (o % 3) + 64)
        for d in range(8):
            to = 15 - (8 * (d // 4) + 4 * (o // 3) + d % 4)
            keep[to, rows, :] = own[64 * d : 64 * d + 64]
            send[to, rows, :] = other[64 * d : 64 * d + 64]


def fetch_kernel(first, after, slab_hbm, slab_rows, sems):
    del after
    copies = [
        pltpu.make_async_copy(slab_hbm.at[first + i], slab_rows.at[i], sems.at[i])
        for i in range(slab_rows.shape[0])
    ]
    for copy in copies:
        copy.start()
    for copy in copies:
        copy.wait()


def insert_kernel(own, across, beside, corner, early, late, tables, out, rows_all, spectrum):
    side, core = lax.axis_index("xl"), lax.axis_index("co")
    rows_all[side, core] = own[...]
    rows_all[side, 1 - core] = across[...]
    rows_all[1 - side, core] = beside[...]
    rows_all[1 - side, 1 - core] = corner[...]
    for plane in range(8):
        found = jnp.zeros((64, N), F32)
        for o in range(ORIENT):
            rows = slice(64 * (o % 3), 64 * (o % 3) + 64)
            factor = jnp.concatenate([rows_all[o // 3, c, rows, :] for c in range(2)], axis=1)
            found += rows_dot(factor, (early[o, plane] if o < EARLY else late[o - EARLY, plane]))
        start = (plane // 4) * 128 + plane % 4
        for part in range(4):
            rows, lanes = 32 * (part // 2), 128 * (part % 2)
            spectrum[part, pl.ds(start, 32, stride=4), :] = found[
                rows : rows + 32, lanes : lanes + 128
            ]
    lane = lax.broadcasted_iota(jnp.int32, (128, 128), 1)
    both = jnp.concatenate([spectrum[part] for part in range(4)], axis=1).astype(BF16)
    result = plain_dot(both, tables[1]) + plain_dot(both, tables[2])
    for e in range(4):
        early = result[:128, 128 * e : 128 * e + 128]
        late = result[128:, 128 * e : 128 * e + 128]
        even = jnp.where(lane < 64, early, pltpu.roll(late, 64, 1))
        odd = jnp.where(lane < 64, pltpu.roll(early, 64, 1), late)
        out[7 - 2 * e] = even.astype(BF16)
        out[6 - 2 * e] = odd.astype(BF16)


def last_kernel(pencils, z_high, z_low, out):
    scaling = 1.0 / (N**1.5 * math.sqrt(2048))
    rows = []
    for d in range(8):
        turned = pencils[d].astype(F32).T.astype(BF16)
        rows.append(jnp.concatenate([turned[32 * q : 32 * q + 32] for q in range(4)], axis=1))
    stacked = jnp.concatenate(rows, axis=0)
    result = plain_dot(stacked, z_high[...]) + plain_dot(stacked, z_low[...])
    for d in range(8):
        out[7 - d] = result[32 * d : 32 * d + 32] * scaling


VMEM_SPEC = pl.BlockSpec(memory_space=pltpu.VMEM)
HBM_SPEC = pl.BlockSpec(memory_space=pltpu.HBM)
FRONT_LIMIT = 53500 * 1024
TOTAL_LIMIT = 8192 * 1024
FETCH_LIMIT = 48500 * 1024
INSERT_LIMIT = 44000 * 1024
LAST_LIMIT = 32768 * 1024


def swap(array, bits):
    return lax.ppermute(array, ("xl", "co"), [(i, i ^ bits) for i in range(4)])


def exchange(array, axes):
    count = array.shape[0]
    return lax.all_to_all(
        array,
        axes,
        split_axis=0,
        concat_axis=0,
        tiled=True,
        axis_index_groups=[list(range(count - 1, -1, -1))],
    )


def fetch(first, count, after, slab_rows):
    return pl.pallas_call(
        functools.partial(fetch_kernel, first),
        out_shape=jax.ShapeDtypeStruct((count, *slab_rows.shape[1:]), BF16),
        in_specs=[VMEM_SPEC, HBM_SPEC],
        out_specs=VMEM_SPEC,
        scratch_shapes=[pltpu.SemaphoreType.DMA((count,))],
        compiler_params=pltpu.CompilerParams(vmem_limit_bytes=FETCH_LIMIT),
        cost_estimate=pl.CostEstimate(
            flops=0, bytes_accessed=2_000_000 * count, transcendentals=0
        ),
        name="fetch",
    )(after, slab_rows)


def total_kernel(pieces, fetched, out):
    del fetched
    sums = pieces[0].astype(F32)
    for i in range(1, pieces.shape[0]):
        sums += pieces[i].astype(F32)
    out[...] = sums.astype(BF16)


def total_of(pieces):
    return jnp.sum(pieces.astype(F32), axis=0).astype(BF16)


def on_device(images, orient_ids, shift_ids, group_ids, translations, defocus, in_plane, slab_rows):
    tables = jnp.asarray(np.stack([x_table()[0], *y_table()]))
    spread = ((0, 1), (16, 8))
    scalars = (
        jnp.pad(translations.T, ((0, 0), (0, 16)))
        + jnp.pad(orient_ids[None], spread).astype(F32)
        + jnp.pad(shift_ids[None], spread).astype(F32) * 8.0
        + jnp.pad(group_ids[None], spread).astype(F32) * 128.0
        + jnp.pad(defocus[None], ((0, 1), (24, 0)))
    )
    keep, send = pl.pallas_call(
        front_kernel,
        out_shape=[
            jax.ShapeDtypeStruct((16, 192, 128), BF16),
            jax.ShapeDtypeStruct((16, 192, 128), BF16),
        ],
        in_specs=[HBM_SPEC] * 4,
        out_specs=[VMEM_SPEC] * 2,
        scratch_shapes=[
            pltpu.VMEM((ORIENT, N, 2 * N), F32),
            pltpu.VMEM((IMG, N, 2 * N), BF16),
            pltpu.VMEM((ORIENT, N, N), BF16),
            pltpu.VMEM((512, 512), BF16),
            pltpu.SMEM((2, 32), F32),
            pltpu.SemaphoreType.DMA((3,)),
            pltpu.SemaphoreType.DMA((IMG,)),
        ],
        compiler_params=pltpu.CompilerParams(vmem_limit_bytes=FRONT_LIMIT),
        name="front",
    )(
        scalars, images, in_plane, tables,
    )
    other = lax.ppermute(send, "co", [(0, 1), (1, 0)])
    pair = (keep.astype(F32) + other.astype(F32)).astype(BF16)
    pieces = exchange(pair, ("xh", "xl", "yy"))
    part = total_of(pieces)
    copies = jnp.broadcast_to(part[None], (8, 192, 128))
    pieces = exchange(copies, "zz")
    early = fetch(0, EARLY, copies, slab_rows)
    own = pl.pallas_call(
        total_kernel,
        out_shape=jax.ShapeDtypeStruct((192, 128), BF16),
        in_specs=[VMEM_SPEC, pl.BlockSpec(memory_space=pl.ANY)],
        out_specs=VMEM_SPEC,
        compiler_params=pltpu.CompilerParams(vmem_limit_bytes=TOTAL_LIMIT),
        name="total",
    )(pieces, early)
    late = fetch(EARLY, ORIENT - EARLY, own, slab_rows)
    sent = pl.pallas_call(
        insert_kernel,
        out_shape=jax.ShapeDtypeStruct((8, 128, 128), BF16),
        in_specs=[VMEM_SPEC] * 7,
        out_specs=VMEM_SPEC,
        scratch_shapes=[
            pltpu.VMEM((2, 2, 192, 128), BF16),
            pltpu.VMEM((4, N, 128), F32),
        ],
        compiler_params=pltpu.CompilerParams(vmem_limit_bytes=INSERT_LIMIT),
        name="insert",
    )(own, swap(own, 1), swap(own, 2), swap(own, 3), early, late, tables)
    pencils = exchange(sent.reshape(256, 4, 128), ALL)
    z_high, z_low = z_table()
    return pl.pallas_call(
        last_kernel,
        out_shape=jax.ShapeDtypeStruct((8, 32, N), F32),
        in_specs=[VMEM_SPEC] * 3,
        out_specs=VMEM_SPEC,
        compiler_params=pltpu.CompilerParams(vmem_limit_bytes=LAST_LIMIT),
        name="last",
    )(pencils.reshape(8, 128, 128), jnp.asarray(z_high), jnp.asarray(z_low))


def solution(mesh):
    fine = Mesh(mesh.devices.reshape(2, 4, 8, 2, 2), ALL)
    return jax.shard_map(
        on_device,
        mesh=fine,
        in_specs=(
            P(ALL, None, None),
            P(ALL),
            P(ALL),
            P(ALL),
            P(),
            P(),
            P(),
            P(None, SLAB, None, None),
        ),
        out_specs=P(SLAB, DOM, None),
        check_vma=False,
    )
```

```python
import math

import jax
import jax.numpy as jnp
import numpy as np
from jax import lax
from jax.experimental import pallas as pl
from jax.experimental.pallas import tpu as pltpu
from jax.sharding import Mesh
from jax.sharding import PartitionSpec as P

N = 256
ORIENT = 6
IMG = 8
WAIT = 4
BF16 = jnp.bfloat16
F32 = jnp.float32

DOM = ("xh", "yy")
SLAB = ("zz", "xl", "co")
ALL = DOM + SLAB


def split_table(table):
    high = table.astype(jnp.bfloat16)
    low = (table - high.astype(np.float64)).astype(jnp.bfloat16)
    return high, low


def phases(left, right):
    angles = (np.outer(left, right) % N) * (2.0 * math.pi / N)
    return np.cos(angles), np.sin(angles)


def x_table():
    x_of = (8 * np.arange(31, -1, -1)[None, :] + np.arange(8)[:, None]).reshape(-1)
    cosine, sine = (t.reshape(8, 32, N) for t in phases(x_of, np.arange(N)))
    real_rows = np.concatenate([cosine, -sine], axis=2)
    imag_rows = np.concatenate([sine, cosine], axis=2)
    return split_table(np.stack([real_rows, imag_rows], axis=1).reshape(512, 512))


def y_table():
    cosine, sine = (t.reshape(N, 8, 32) for t in phases(np.arange(N), np.arange(N)))
    from_real = np.stack([cosine, sine], axis=2).reshape(N, 512)
    from_imag = np.stack([-sine, cosine], axis=2).reshape(N, 512)
    return split_table(np.concatenate([from_real, from_imag], axis=0))


def z_table():
    half, slab, part = np.meshgrid(np.arange(2), np.arange(31, -1, -1), np.arange(4), indexing="ij")
    kz_of = (8 * slab + 4 * half + part).reshape(-1)
    cosine, sine = (t.reshape(2, 128, N) for t in phases(kz_of, np.arange(N)))
    return split_table(np.stack([cosine, -sine], axis=1).reshape(512, N))


def rows_dot(left, right):
    return lax.dot_general(left, right, (((1,), (1,)), ((), ())), preferred_element_type=F32)


def plain_dot(left, right):
    return jnp.dot(left, right, preferred_element_type=F32)


def front_kernel(
    scalars_in, images_hbm, in_plane_hbm, tables,
    keep, send,
    total, images, in_plane, x_rows, scalars, big_sems, image_sems,
):
    scalar_copy = pltpu.make_async_copy(scalars_in, scalars, big_sems.at[2])
    scalar_copy.start()
    image_copies = [
        pltpu.make_async_copy(images_hbm.at[p], images.at[p], image_sems.at[p]) for p in range(IMG)
    ]
    for copy in image_copies:
        copy.start()
    plane_copy = pltpu.make_async_copy(in_plane_hbm, in_plane, big_sems.at[0])
    table_copy = pltpu.make_async_copy(tables.at[0], x_rows, big_sems.at[1])
    total[...] = jnp.zeros_like(total)
    scalar_copy.wait()
    position = lax.broadcasted_iota(jnp.int32, (IMG, N), 1)
    freq = jnp.where(position < N // 2, position, position - N).astype(F32)
    row = lax.broadcasted_iota(jnp.int32, (IMG, N), 0)
    shift_y = jnp.zeros((IMG, N), F32)
    shift_x = jnp.zeros((IMG, N), F32)
    focus = jnp.zeros((IMG, N), F32)
    classes = []
    for p in range(IMG):
        code = scalars[0, 16 + p].astype(jnp.int32)
        shift, group = (code // 8) % 16, code // 128
        classes.append(code % 8)
        shift_y = jnp.where(row == p, scalars[0, shift], shift_y)
        shift_x = jnp.where(row == p, scalars[1, shift], shift_x)
        focus = jnp.where(row == p, scalars[0, 24 + group], focus)
    squares = freq * freq * (1.0 / (N // 2) ** 2)
    step = 2.0 * math.pi / N
    angles = jnp.concatenate(
        [
            step * shift_y * freq,
            focus * squares + 0.1,
            step * shift_x * freq,
            focus * squares,
        ],
        axis=0,
    )
    sines = jnp.sin(angles)
    cosines = jnp.cos(angles)
    columns = jnp.concatenate([sines, cosines, jnp.zeros((64, N), F32)], axis=0).T
    chunk = 32
    for p in range(IMG):
        if p % WAIT == 0:
            for copy in image_copies[p : p + WAIT]:
                copy.wait()
        if p == 0:
            plane_copy.start()
            table_copy.start()
        sin_tx, sin_fx = sines[16 + p : 17 + p], sines[24 + p : 25 + p]
        cos_tx, cos_fx = cosines[16 + p : 17 + p], cosines[24 + p : 25 + p]
        which = classes[p]
        for r in range(0, N, chunk):
            rows = slice(r, r + chunk)
            sin_ty = columns[rows, p : p + 1]
            sin_fy = columns[rows, 8 + p : 9 + p]
            cos_ty = columns[rows, 32 + p : 33 + p]
            cos_fy = columns[rows, 40 + p : 41 + p]
            contrast = -(sin_fy * cos_fx + cos_fy * sin_fx)
            turn_re = contrast * (cos_ty * cos_tx - sin_ty * sin_tx)
            turn_im = contrast * (sin_ty * cos_tx + cos_ty * sin_tx)
            real_part = images[p, rows, :N].astype(F32)
            imag_part = images[p, rows, N:].astype(F32)
            total[which, rows, :N] += real_part * turn_re + imag_part * turn_im
            total[which, rows, N:] += imag_part * turn_re - real_part * turn_im
    first = lax.axis_index("co") == 0
    plane_copy.wait()
    table_copy.wait()
    for o in range(ORIENT):
        sums = total[o].astype(BF16)
        matrix = in_plane[o]
        mixed = jnp.concatenate(
            [plain_dot(sums[:, :N], matrix), plain_dot(sums[:, N:], matrix)], axis=1
        ).astype(BF16)
        along = rows_dot(x_rows[...], mixed).astype(BF16)
        low_half, high_half = along[:, :128], along[:, 128:]
        own = jnp.where(first, low_half, high_half)
        other = jnp.where(first, high_half, low_half)
        rows = slice(64 * (o % 3), 64 * (o % 3) + 64)
        for d in range(8):
            to = 15 - (8 * (d // 4) + 4 * (o // 3) + d % 4)
            keep[to, rows, :] = own[64 * d : 64 * d + 64]
            send[to, rows, :] = other[64 * d : 64 * d + 64]


def fetch_kernel(after, slab_hbm, slab_rows, sems):
    del after
    copies = [
        pltpu.make_async_copy(
            slab_hbm.at[o, pl.ds(4 * half, 4)], slab_rows.at[o, pl.ds(4 * half, 4)], sems.at[2 * o + half]
        )
        for o in range(ORIENT)
        for half in range(2)
    ]
    for copy in copies:
        copy.start()
    for copy in copies:
        copy.wait()


def insert_kernel(own, across, beside, corner, slab_rows, tables, out, rows_all, spectrum):
    side, core = lax.axis_index("xl"), lax.axis_index("co")
    rows_all[side, core] = own[...]
    rows_all[side, 1 - core] = across[...]
    rows_all[1 - side, core] = beside[...]
    rows_all[1 - side, 1 - core] = corner[...]
    for plane in range(8):
        found = jnp.zeros((64, N), F32)
        for o in range(ORIENT):
            rows = slice(64 * (o % 3), 64 * (o % 3) + 64)
            factor = jnp.concatenate([rows_all[o // 3, c, rows, :] for c in range(2)], axis=1)
            found += rows_dot(factor, slab_rows[o, plane])
        start = (plane // 4) * 128 + plane % 4
        for part in range(4):
            rows, lanes = 32 * (part // 2), 128 * (part % 2)
            spectrum[part, pl.ds(start, 32, stride=4), :] = found[
                rows : rows + 32, lanes : lanes + 128
            ]
    lane = lax.broadcasted_iota(jnp.int32, (128, 128), 1)
    both = jnp.concatenate([spectrum[part] for part in range(4)], axis=1).astype(BF16)
    result = plain_dot(both, tables[0]) + plain_dot(both, tables[1])
    for e in range(4):
        early = result[:128, 128 * e : 128 * e + 128]
        late = result[128:, 128 * e : 128 * e + 128]
        even = jnp.where(lane < 64, early, pltpu.roll(late, 64, 1))
        odd = jnp.where(lane < 64, pltpu.roll(early, 64, 1), late)
        out[7 - 2 * e] = even.astype(BF16)
        out[6 - 2 * e] = odd.astype(BF16)


def last_kernel(pencils, z_high, z_low, out):
    scaling = 1.0 / (N**1.5 * math.sqrt(2048))
    rows = []
    for d in range(8):
        turned = pencils[d].astype(F32).T.astype(BF16)
        rows.append(jnp.concatenate([turned[32 * q : 32 * q + 32] for q in range(4)], axis=1))
    stacked = jnp.concatenate(rows, axis=0)
    result = plain_dot(stacked, z_high[...]) + plain_dot(stacked, z_low[...])
    for d in range(8):
        out[7 - d] = result[32 * d : 32 * d + 32] * scaling


VMEM_SPEC = pl.BlockSpec(memory_space=pltpu.VMEM)
HBM_SPEC = pl.BlockSpec(memory_space=pltpu.HBM)
FRONT_LIMIT = 53500 * 1024
FETCH_LIMIT = 44000 * 1024
INSERT_LIMIT = 44000 * 1024
LAST_LIMIT = 32768 * 1024


def swap(array, bits):
    return lax.ppermute(array, ("xl", "co"), [(i, i ^ bits) for i in range(4)])


def exchange(array, axes):
    count = array.shape[0]
    return lax.all_to_all(
        array,
        axes,
        split_axis=0,
        concat_axis=0,
        tiled=True,
        axis_index_groups=[list(range(count - 1, -1, -1))],
    )


def total_of(pieces):
    return jnp.sum(pieces.astype(F32), axis=0).astype(BF16)


def on_device(images, orient_ids, shift_ids, group_ids, translations, defocus, in_plane, slab_rows):
    tables = jnp.asarray(np.stack([x_table()[0], *y_table()]))
    spread = ((0, 1), (16, 8))
    scalars = (
        jnp.pad(translations.T, ((0, 0), (0, 16)))
        + jnp.pad(orient_ids[None], spread).astype(F32)
        + jnp.pad(shift_ids[None], spread).astype(F32) * 8.0
        + jnp.pad(group_ids[None], spread).astype(F32) * 128.0
        + jnp.pad(defocus[None], ((0, 1), (24, 0)))
    )
    keep, send = pl.pallas_call(
        front_kernel,
        out_shape=[
            jax.ShapeDtypeStruct((16, 192, 128), BF16),
            jax.ShapeDtypeStruct((16, 192, 128), BF16),
        ],
        in_specs=[HBM_SPEC] * 4,
        out_specs=[VMEM_SPEC] * 2,
        scratch_shapes=[
            pltpu.VMEM((ORIENT, N, 2 * N), F32),
            pltpu.VMEM((IMG, N, 2 * N), BF16),
            pltpu.VMEM((ORIENT, N, N), BF16),
            pltpu.VMEM((512, 512), BF16),
            pltpu.SMEM((2, 32), F32),
            pltpu.SemaphoreType.DMA((3,)),
            pltpu.SemaphoreType.DMA((IMG,)),
        ],
        compiler_params=pltpu.CompilerParams(vmem_limit_bytes=FRONT_LIMIT),
        name="front",
    )(
        scalars, images, in_plane, tables,
    )
    other = lax.ppermute(send, "co", [(0, 1), (1, 0)])
    pair = (keep.astype(F32) + other.astype(F32)).astype(BF16)
    pieces = exchange(pair, ("xh", "xl", "yy"))
    part = total_of(pieces)
    pieces = exchange(jnp.broadcast_to(part[None], (8, 192, 128)), "zz")
    own = total_of(pieces)
    fetched = pl.pallas_call(
        fetch_kernel,
        out_shape=jax.ShapeDtypeStruct(slab_rows.shape, BF16),
        in_specs=[VMEM_SPEC, HBM_SPEC],
        out_specs=VMEM_SPEC,
        scratch_shapes=[pltpu.SemaphoreType.DMA((2 * ORIENT,))],
        compiler_params=pltpu.CompilerParams(vmem_limit_bytes=FETCH_LIMIT),
        cost_estimate=pl.CostEstimate(flops=0, bytes_accessed=12_000_000, transcendentals=0),
        name="fetch",
    )(own, slab_rows)
    sent = pl.pallas_call(
        insert_kernel,
        out_shape=jax.ShapeDtypeStruct((8, 128, 128), BF16),
        in_specs=[VMEM_SPEC] * 6,
        out_specs=VMEM_SPEC,
        scratch_shapes=[
            pltpu.VMEM((2, 2, 192, 128), BF16),
            pltpu.VMEM((4, N, 128), F32),
        ],
        compiler_params=pltpu.CompilerParams(vmem_limit_bytes=INSERT_LIMIT),
        name="insert",
    )(own, swap(own, 1), swap(own, 2), swap(own, 3), fetched, jnp.asarray(np.stack(y_table())))
    pencils = exchange(sent.reshape(256, 4, 128), ALL)
    z_high, z_low = z_table()
    return pl.pallas_call(
        last_kernel,
        out_shape=jax.ShapeDtypeStruct((8, 32, N), F32),
        in_specs=[VMEM_SPEC] * 3,
        out_specs=VMEM_SPEC,
        compiler_params=pltpu.CompilerParams(vmem_limit_bytes=LAST_LIMIT),
        name="last",
    )(pencils.reshape(8, 128, 128), jnp.asarray(z_high), jnp.asarray(z_low))


def solution(mesh):
    fine = Mesh(mesh.devices.reshape(2, 4, 8, 2, 2), ALL)
    return jax.shard_map(
        on_device,
        mesh=fine,
        in_specs=(
            P(ALL, None, None),
            P(ALL),
            P(ALL),
            P(ALL),
            P(),
            P(),
            P(),
            P(None, SLAB, None, None),
        ),
        out_specs=P(SLAB, DOM, None),
        check_vma=False,
    )
```
